128 devices in a mesh: axial: 4 (over z), sector: 16 (over y_lo, x, core), modes: 2 (over y_hi).
Axes of the slice: x: 4, y: 4 (y_hi: 2, y_lo: 2; y = y_hi * 2 + y_lo), z: 4, core: 2. Of those that a mesh axis runs over, the one named last changes fastest.
Arguments:
- rhs: float32 [2, 8, 64, 128, 256], P(None, 'modes', 'axial', 'sector'), may hold values from -8 to 8
- adjoint_start: float32 [2, 8, 64, 128, 256], P(None, 'modes', 'axial', 'sector'), may hold values from -8 to 8
- sound_sq: float32 [64, 128, 256], P('axial', 'sector'), may hold values from 0.25 to 4
- direct_mode: bfloat16 [2, 8, 64, 128, 256], P(None, 'modes', 'axial', 'sector'), may hold values from -6 to 6
- omega_sq: float32 [2, 8], P(None, 'modes'), may hold values from 0.5 to 3
- flame_gain: float32 [4, 8192], P('axial', 'sector'), may hold values from 1 to 8
- delay_phase: float32 [8, 32], P('modes'), may hold values from -3.140625 to 3.140625
- delay_bin: int32 [4, 8192], P('axial', 'sector'), may hold values from 0 to 31
- flame_cell: int32 [4, 8192], P('axial', 'sector'), may hold values from 0 to 32767
- injector_sector: int32 [4, 8192, 1], P('axial', 'sector'), may hold values from 0 to 15; in each aligned block of 512 rows (0 to 511, 512 to 1023, ..., all dimensions but the last counted through in order) at most 96 rows name the same one
- injector_cell: int32 [4, 8192], P('axial', 'sector'), may hold values from 0 to 32767
Outputs:
- adjoint: float32 [2, 8, 64, 128, 256], P(None, 'modes', 'axial', 'sector')
- sensitivity: float32 [64, 128, 256], P('axial', 'sector')
The draws below stay inside these ranges and needn't reach their ends.
Inputs may be any that keep to these rules, and one draw needn't show every extreme that they name: `injector_sector`: among the flame cells of one device (each aligned block of 512 along 8192), at most 96 name the same sector, a bound that some block reaches.
All inputs are finite; a program needn't handle non-finite values.
Results may differ from the reference program's by a relative error of at most 0.0003.
Values sent between devices are 32-bit elements; how exact they have to be, the bound alone decides.
A program may use at most 128 MiB of HBM per device.

```python
import math
import jax
import jax.numpy as jnp
import numpy as np

CA = 16
CT = 8
CR = 256
MODES = 8
NBINS = 32
ITERS = 2
FL_DEV = 512
CAP = 96
NAX = 64
NTH = 128
SLABS = 4
FLAMES = 8192
N_SECTOR = 16


def with_ends(result, stream_key, least, high):
    place = [jax.random.randint(jax.random.fold_in(stream_key, axis), (), 0, length) for axis, length in enumerate(result.shape)]
    main_axis = result.shape.index(max(result.shape))
    next_to = place[:main_axis] + [(place[main_axis] + 1) % result.shape[main_axis]] + place[main_axis + 1:]
    return result.at[tuple(place)].set(least).at[tuple(next_to)].set(high)


def levels(key, shape, shards, smallest, largest):
    def one(position, parts):
        draws = jax.random.uniform(jax.random.fold_in(jax.random.fold_in(key, 6), position), (parts,), jnp.float32, smallest / len(shards), largest / len(shards))
        return jnp.repeat(jnp.exp(draws), shape[position] // parts).reshape((-1,) + (1,) * (len(shape) - position - 1))

    factor_of = one(*shards[0])
    for cut in shards[1:]:
        factor_of = factor_of * one(*cut)
    return factor_of


def routed_block(key, own, number, rows, number_of, top, most, lean):
    order = jax.random.permutation(key, number_of)
    heavy_load, usual = shares(number_of, rows * top, most, lean, True), shares(number_of, rows * top, most, lean, False)
    places = jnp.arange(number_of)

    def named(lengths, rotation):
        used = int((lengths > 0).sum())
        fixed = max(1, used // 4)
        passed = fixed + (places - fixed + rotation * (used - fixed)) % max(1, number_of - fixed)
        return jnp.zeros((number_of,), jnp.int32).at[order[jnp.where(places < fixed, places, passed)]].set(jnp.asarray(lengths, jnp.int32))

    lengths = jnp.where(number % 4 == 0, named(heavy_load, number // 4), named(usual, number - number // 4 - 1))
    mixed = jax.random.permutation(jax.random.fold_in(own, 3), number_of)
    giver, sink = mixed[0:number_of // 2 * 2:2], mixed[1:number_of // 2 * 2:2]
    room = jnp.minimum(lengths[giver] - 1, most - lengths[sink]) // 2
    room = jnp.where((giver == order[0]) | (sink == order[0]) | (lengths[sink] == 0), 0, jnp.maximum(room, 0))
    passed = jax.random.randint(jax.random.fold_in(own, 4), (number_of // 2,), 0, 1 << 20) % (room + 1)
    lengths = lengths.at[giver].add(-passed).at[sink].add(passed)
    items = jnp.searchsorted(jnp.cumsum(lengths), jnp.arange(rows * top), side="right").astype(jnp.int32)
    grid = items.reshape(top, rows).T
    grid = grid[jax.random.permutation(jax.random.fold_in(own, 1), rows)]
    rotation = jax.random.randint(jax.random.fold_in(own, 2), (rows, 1), 0, top)
    return jnp.take_along_axis(grid, (jnp.arange(top)[None, :] + rotation) % top, axis=1)


def shares(count, total, limit, skew, full):
    loads = [(1 << 20) // math.isqrt(rank ** skew) + 1 for rank in range(1, count + 1)]
    largest = limit if full else min(limit, max(-(-total // count), total * loads[0] // sum(loads)))
    least = 1 if total - largest >= count - 1 else 0
    counts, spare = [largest] + [least] * (count - 1), total - largest - least * (count - 1)
    while spare > 0:
        candidates = [i for i in range(1, count) if counts[i] < largest] or [i for i in range(1, count) if counts[i] < limit]
        whole, remaining = sum([loads[i] for i in candidates]), spare
        for i in candidates:
            extra = min(limit - counts[i], max(1, remaining * loads[i] // whole), spare)
            counts[i] = counts[i] + extra
            spare = spare - extra
    return np.array(counts)


def normal_values(stream_key, dims, deviation, reach, pieces=(), kind=jnp.bfloat16):
    array = deviation * jax.random.normal(stream_key, dims, jnp.float32)
    if pieces:
        array = array * levels(stream_key, dims, pieces, -0.22, 0.18)
    return jnp.clip(array, -reach, reach).astype(kind)


def setup_inputs(seed: int = 0) -> dict:
    key_list = jax.random.split(jax.random.key(seed), 12)
    rhs = normal_values(key_list[0], (2, MODES, NAX, NTH, CR), 1.0, 8.0, ((1, 2), (2, 4), (3, 16)), jnp.float32)
    adjoint_start = normal_values(key_list[1], (2, MODES, NAX, NTH, CR), 1.0, 8.0, ((1, 2), (2, 4), (3, 16)), jnp.float32)
    sound_sq = jnp.clip(jnp.exp(math.log(4.0) - 2.7725887 * jax.random.uniform(key_list[2], (NAX, NTH, CR), jnp.float32) ** levels(key_list[2], (NAX, NTH, CR), ((0, 4), (1, 16)), -0.2, 0.2)), 0.25, 4.0)
    direct_mode = normal_values(key_list[3], (2, MODES, NAX, NTH, CR), 1.0, 6.0, ((1, 2), (2, 4), (3, 16)))
    omega_sq = jnp.clip(0.5 + 2.5 * jax.random.uniform(key_list[4], (2, MODES), jnp.float32) ** levels(key_list[4], (2, MODES), ((1, 2),), -0.2, 0.2), 0.5, 3.0)
    flame_gain = jnp.clip(jnp.exp(math.log(8.0) - 2.0794415 * jax.random.uniform(key_list[5], (SLABS, FLAMES), jnp.float32) ** levels(key_list[5], (SLABS, FLAMES), ((0, 4), (1, 16)), -0.2, 0.2)), 1.0, 8.0)
    delay_phase = jnp.clip(jax.random.uniform(key_list[6], (MODES, NBINS), jnp.float32, -3.140625, 3.140625), -3.140625, 3.140625)
    delay_bin = with_ends(jax.random.randint(key_list[7], (SLABS, FLAMES), 0, NBINS), jax.random.fold_in(key_list[7], 1), 0, NBINS - 1).astype(jnp.int32)
    flame_cell = with_ends(jax.random.randint(key_list[8], (SLABS, FLAMES), 0, CA * CT * CR), jax.random.fold_in(key_list[8], 1), 0, (CA * CT * CR) - 1).astype(jnp.int32)
    injector_sector_keys = jax.random.split(jax.random.fold_in(key_list[9], 1), SLABS * FLAMES // FL_DEV)
    injector_sector_turns = jax.random.permutation(jax.random.fold_in(key_list[9], 3), SLABS * FLAMES // FL_DEV)
    injector_sector = jax.vmap(lambda own, number: routed_block(jax.random.fold_in(key_list[9], 2), own, number, FL_DEV, N_SECTOR, 1, CAP, 2))(injector_sector_keys, injector_sector_turns).reshape((SLABS, FLAMES, 1))
    injector_cell = with_ends(jax.random.randint(key_list[10], (SLABS, FLAMES), 0, CA * CT * CR), jax.random.fold_in(key_list[10], 1), 0, (CA * CT * CR) - 1).astype(jnp.int32)
    return dict(rhs=rhs, adjoint_start=adjoint_start, sound_sq=sound_sq, direct_mode=direct_mode, omega_sq=omega_sq, flame_gain=flame_gain, delay_phase=delay_phase, delay_bin=delay_bin, flame_cell=flame_cell, injector_sector=injector_sector, injector_cell=injector_cell)


relax_weight = 0.6


def couple(values, speeds, val_alo, val_ahi, spd_alo, spd_ahi, val_slo, val_shi, spd_slo, spd_shi):
    k_alo = 0.5 * (speeds + spd_alo)
    k_ahi = 0.5 * (speeds + spd_ahi)
    k_slo = 0.5 * (speeds + spd_slo)
    k_shi = 0.5 * (speeds + spd_shi)
    applied = k_alo * (values - val_alo) + k_ahi * (values - val_ahi)
    applied = applied + k_slo * (values - val_slo) + k_shi * (values - val_shi)
    weights = k_alo + k_ahi + k_slo + k_shi
    k_radial = 0.5 * (speeds[..., 1:] + speeds[..., :-1])
    radial_flux = k_radial * (values[..., 1:] - values[..., :-1])
    value_lo = [(0, 0)] * (values.ndim - 1) + [(1, 0)]
    value_hi = [(0, 0)] * (values.ndim - 1) + [(0, 1)]
    speed_lo = [(0, 0)] * (speeds.ndim - 1) + [(1, 0)]
    speed_hi = [(0, 0)] * (speeds.ndim - 1) + [(0, 1)]
    applied = applied + jnp.pad(radial_flux, value_lo) - jnp.pad(radial_flux, value_hi)
    weights = weights + jnp.pad(k_radial, speed_lo) + jnp.pad(k_radial, speed_hi)
    return applied, weights


def flame_sources(fields, flame_gain, delay_phase, delay_bin, flame_cell, injector_sector, injector_cell):
    slab_ids = jnp.arange(SLABS, dtype=jnp.int32)[:, None]
    column_ids = jnp.arange(FLAMES, dtype=jnp.int32)[None, :]
    source_sector = column_ids // FL_DEV

    def global_index(sector_ids, local_ids):
        axial_pos = local_ids // (CT * CR)
        azimuth_pos = (local_ids // CR) % CT
        radial_pos = local_ids % CR
        return ((slab_ids * CA + axial_pos) * NTH + sector_ids * CT + azimuth_pos) * CR + radial_pos

    sources = global_index(source_sector, flame_cell).reshape(-1).astype(jnp.int32)
    targets = global_index(injector_sector[:, :, 0], injector_cell).reshape(-1).astype(jnp.int32)
    flat_fields = fields.reshape(2, MODES, -1)
    picked = flat_fields[:, :, sources]
    bins = delay_bin.reshape(-1)
    cosines = jnp.cos(delay_phase)[:, bins]
    sines = -jnp.sin(delay_phase)[:, bins]
    gains = flame_gain.reshape(-1)[None, :]
    real_part = gains * (cosines * picked[0] - sines * picked[1])
    imag_part = gains * (cosines * picked[1] + sines * picked[0])
    totals = jnp.zeros((2, MODES, NAX * NTH * CR), jnp.float32)
    return totals.at[:, :, targets].add(jnp.stack([real_part, imag_part]))


def reference(rhs, adjoint_start, sound_sq, direct_mode, omega_sq, flame_gain, delay_phase, delay_bin, flame_cell, injector_sector, injector_cell):
    fields = adjoint_start
    speeds = sound_sq
    zero_values = jnp.zeros((2 * MODES, 1, NTH, CR), jnp.float32)
    zero_speeds = jnp.zeros((1, NTH, CR), jnp.float32)
    spd_alo = jnp.concatenate([zero_speeds, speeds[:-1]], 0)
    spd_ahi = jnp.concatenate([speeds[1:], zero_speeds], 0)
    spd_slo = jnp.roll(speeds, 1, axis=1)
    spd_shi = jnp.roll(speeds, -1, axis=1)
    w_real = omega_sq[0][:, None, None, None]
    w_imag = omega_sq[1][:, None, None, None]
    for step_index in range(ITERS):
        values = fields.reshape(2 * MODES, NAX, NTH, CR)
        val_alo = jnp.concatenate([zero_values, values[:, :-1]], 1)
        val_ahi = jnp.concatenate([values[:, 1:], zero_values], 1)
        val_slo = jnp.roll(values, 1, axis=2)
        val_shi = jnp.roll(values, -1, axis=2)
        applied, weights = couple(values, speeds, val_alo, val_ahi, spd_alo, spd_ahi, val_slo, val_shi, spd_slo, spd_shi)
        applied = applied.reshape(2, MODES, NAX, NTH, CR)
        injected = flame_sources(fields, flame_gain, delay_phase, delay_bin, flame_cell, injector_sector, injector_cell)
        injected = injected.reshape(2, MODES, NAX, NTH, CR)
        mass_real = w_real * fields[0] - w_imag * fields[1]
        mass_imag = w_real * fields[1] + w_imag * fields[0]
        operated = applied - jnp.stack([mass_real, mass_imag]) + injected
        fields = fields + relax_weight * (rhs - operated) / weights
    direct_values = direct_mode.astype(jnp.float32)
    sensitivity = jnp.sum(fields[0] * direct_values[0] - fields[1] * direct_values[1], axis=0)
    return fields, sensitivity
```

```python
import functools

import jax
import jax.numpy as jnp
from jax import lax
from jax.experimental import pallas as pl
from jax.experimental.pallas import tpu as pltpu
from jax.sharding import PartitionSpec as P

ITERS = 2
RELAX = 0.6
CAP = 96
LANES = 128
MESH = pl.DeviceIdType.MESH
BF16 = jnp.bfloat16
F32 = jnp.float32
I32 = jnp.int32


def one_hot(flags):
    return jnp.where(flags, 1.0, 0.0).astype(BF16)


def halves(values):
    high = values.astype(BF16)
    return high, (values - high.astype(F32)).astype(BF16)


def dot_nt(left, right):
    return lax.dot_general(
        left, right, (((1,), (1,)), ((), ())), preferred_element_type=F32
    )


def read(ref, *index):
    *lead, at = index
    tiles = ref.shape[len(lead)]
    return jnp.concatenate([ref[(*lead, i, at)] for i in range(tiles)], axis=-1)


def write(ref, *index_and_value):
    *lead, at, value = index_and_value
    for i in range(ref.shape[len(lead)]):
        ref[(*lead, i, at)] = value[..., i * LANES : (i + 1) * LANES]


def kernel(
    n_sector,
    n_axial,
    shape,
    rhs_hbm,
    start_hbm,
    sound_hbm,
    direct_hbm,
    omega_hbm,
    gain_hbm,
    phase_hbm,
    bin_hbm,
    source_hbm,
    sector_hbm,
    target_hbm,
    adjoint_hbm,
    sens_hbm,
    rhs,
    field_a,
    field_b,
    sound,
    direct,
    omega,
    gain,
    phase,
    bins,
    source,
    sector,
    target,
    result,
    base,
    coef,
    edge,
    pick_radial,
    pick_row,
    lane_hot,
    dist_hot,
    gain_cos,
    gain_sin,
    put_row,
    put_radial,
    sound_send,
    sound_side,
    side_send,
    side_recv,
    cell_send,
    cell_recv,
    flame_send,
    flame_recv,
    sens_own,
    sens_other,
    in_sem,
    out_sem,
    sound_sems,
    halo_sems,
    cell_sems,
    flame_sems,
    sens_sems,
):
    modes, axial_cells, azimuth_cells, radial_cells = shape
    channels = 2 * modes
    rows = axial_cells * azimuth_cells
    flames = gain.shape[1]
    slots = n_sector * CAP
    tiles = radial_cells // LANES
    axial = lax.axis_index("axial")
    my_sector = lax.axis_index("sector")
    my_modes = lax.axis_index("modes")
    up_axial = lax.rem(axial + 1, n_axial)
    down_axial = lax.rem(axial + n_axial - 1, n_axial)

    def sector_at(distance):
        return lax.rem(my_sector + (distance + n_sector), n_sector)

    barrier = pltpu.get_barrier_semaphore()
    for distance in range(1, n_sector):
        pl.semaphore_signal(
            barrier, inc=1, device_id={"sector": sector_at(distance)}, device_id_type=MESH
        )
    for other in (up_axial, down_axial):
        pl.semaphore_signal(barrier, inc=1, device_id={"axial": other}, device_id_type=MESH)
    pl.semaphore_signal(
        barrier, inc=1, device_id={"modes": 1 - my_modes}, device_id_type=MESH
    )

    inner = pl.ds(azimuth_cells, rows)
    loads = [
        pltpu.make_async_copy(a, b, in_sem.at[i])
        for i, (a, b) in enumerate(
            (
                (sector_hbm, sector),
                (target_hbm, target),
                (source_hbm, source),
                (bin_hbm, bins),
                (phase_hbm, phase),
                (gain_hbm, gain),
                (sound_hbm.at[:, pl.ds(0, LANES)], sound.at[0, inner]),
                (sound_hbm.at[:, pl.ds(LANES, LANES)], sound.at[1, inner]),
                (start_hbm.at[:, :, pl.ds(0, LANES)], field_a.at[:, 0, inner]),
                (start_hbm.at[:, :, pl.ds(LANES, LANES)], field_a.at[:, 1, inner]),
                (omega_hbm, omega),
                (rhs_hbm, rhs),
                (direct_hbm, direct),
            )
        )
    ]
    for load in loads:
        load.start()

    for load in loads[:3]:
        load.wait()
    distance_of = lax.rem(sector[...] - my_sector + n_sector, n_sector)
    to_sector = jnp.broadcast_to(distance_of, (n_sector, flames)) == lax.broadcasted_iota(
        I32, (n_sector, flames), 0
    )
    dist_f32 = jnp.where(to_sector, 1.0, 0.0)
    dist_hot[...] = dist_f32
    before = one_hot(
        lax.broadcasted_iota(I32, (flames, flames), 0)
        < lax.broadcasted_iota(I32, (flames, flames), 1)
    )
    earlier = jnp.dot(dist_f32.astype(BF16), before, preferred_element_type=F32)
    rank = jnp.sum(dist_f32 * earlier, axis=0, keepdims=True).astype(I32)
    lane = (rank + CAP * distance_of) & (LANES - 1)
    lane_hot[...] = one_hot(
        lax.broadcasted_iota(I32, (LANES, flames), 0) == jnp.broadcast_to(lane, (LANES, flames))
    )

    def pack(parts):
        left = jnp.concatenate(
            [
                jnp.concatenate(
                    [part * dist_hot[d : d + 1, :] for d in range(n_sector)], axis=0
                ).astype(BF16)
                for part in parts
            ],
            axis=0,
        )
        packed = dot_nt(left, lane_hot[...])
        total = packed[: 8 * n_sector]
        for i in range(1, len(parts)):
            total = total + packed[8 * n_sector * i : 8 * n_sector * (i + 1)]
        return total.reshape(n_sector, 8, LANES)

    target_row = (target[...] // radial_cells).astype(F32)
    target_radial = (target[...] % radial_cells).astype(F32)
    sub = lax.broadcasted_iota(I32, (8, flames), 0)
    cell_send[...] = pack(
        [
            jnp.where(
                sub == 0,
                jnp.broadcast_to(target_row, (8, flames)),
                jnp.where(sub == 1, jnp.broadcast_to(target_radial, (8, flames)), 0.0),
            )
        ]
    )

    loads[6].wait()
    loads[7].wait()
    for side, row in ((0, 0), (1, azimuth_cells - 1)):
        for i in range(tiles):
            sound_send[side, i] = sound[i, pl.ds(azimuth_cells + row, axial_cells, azimuth_cells), :]

    pl.semaphore_wait(barrier, n_sector + 2)

    def axial_halo(ref, sems):
        last = pl.ds(rows, azimuth_cells)
        first = pl.ds(azimuth_cells, azimuth_cells)
        below = pl.ds(0, azimuth_cells)
        above = pl.ds(rows + azimuth_cells, azimuth_cells)
        at = (lambda part: ref.at[:, part]) if len(ref.shape) == 3 else (lambda part: ref.at[:, :, part])
        return [
            pltpu.make_async_remote_copy(
                src_ref=at(last),
                dst_ref=at(below),
                send_sem=sems.at[0, 0],
                recv_sem=sems.at[1, 0],
                device_id={"axial": up_axial},
                device_id_type=MESH,
            ),
            pltpu.make_async_remote_copy(
                src_ref=at(first),
                dst_ref=at(above),
                send_sem=sems.at[0, 1],
                recv_sem=sems.at[1, 1],
                device_id={"axial": down_axial},
                device_id_type=MESH,
            ),
        ]

    def side_halo(send, recv, sems):
        return [
            pltpu.make_async_remote_copy(
                src_ref=send.at[1],
                dst_ref=recv.at[0],
                send_sem=sems.at[0, 2],
                recv_sem=sems.at[1, 2],
                device_id={"sector": sector_at(1)},
                device_id_type=MESH,
            ),
            pltpu.make_async_remote_copy(
                src_ref=send.at[0],
                dst_ref=recv.at[1],
                send_sem=sems.at[0, 3],
                recv_sem=sems.at[1, 3],
                device_id={"sector": sector_at(-1)},
                device_id_type=MESH,
            ),
        ]

    def blocks(send, recv, sems):
        return [
            pltpu.make_async_remote_copy(
                src_ref=send.at[distance],
                dst_ref=recv.at[distance],
                send_sem=sems.at[0, distance],
                recv_sem=sems.at[1, distance],
                device_id={"sector": sector_at(distance)},
                device_id_type=MESH,
            )
            for distance in range(1, n_sector)
        ]

    sends = []

    def start(copies):
        for copy in copies:
            copy.start()
        sends.extend(copies)
        return copies

    sound_copies = start(axial_halo(sound, sound_sems) + side_halo(sound_send, sound_side, sound_sems))
    cell_copies = start(blocks(cell_send, cell_recv, cell_sems))
    cell_recv[0] = cell_send[0]

    def send_sides(field, step):
        for side, row in ((0, 0), (1, azimuth_cells - 1)):
            for c in range(channels):
                for i in range(tiles):
                    side_send[step, side, c, i] = field[
                        c, i, pl.ds(azimuth_cells + row, axial_cells, azimuth_cells), :
                    ]
        sems = halo_sems.at[step]
        return start(
            axial_halo(field, sems) + side_halo(side_send.at[step], side_recv.at[step], sems)
        )

    cell = source[...]
    row_of = jnp.broadcast_to(cell // radial_cells, (rows, flames))
    pick_row[...] = jnp.where(lax.broadcasted_iota(I32, (rows, flames), 0) == row_of, 1.0, 0.0)
    radial_of = jnp.broadcast_to(cell % radial_cells, (radial_cells, flames))
    radial_hot = one_hot(lax.broadcasted_iota(I32, (radial_cells, flames), 0) == radial_of)
    pick_radial[:radial_cells] = radial_hot
    pick_radial[radial_cells:] = radial_hot

    for load in loads[3:6]:
        load.wait()
    bin_count = phase.shape[1]
    bin_hot = jnp.where(
        lax.broadcasted_iota(I32, (bin_count, flames), 0)
        == jnp.broadcast_to(bins[...], (bin_count, flames)),
        1.0,
        0.0,
    )
    angle = phase[...]
    gains = jnp.broadcast_to(gain[...], (modes, flames))
    exact = lax.Precision.HIGHEST
    gain_cos[...] = gains * jnp.dot(
        jnp.cos(angle), bin_hot, precision=exact, preferred_element_type=F32
    )
    gain_sin[...] = -gains * jnp.dot(
        jnp.sin(angle), bin_hot, precision=exact, preferred_element_type=F32
    )

    def send_flames(field, step):
        group = channels // 2
        picked = []
        for g in range(2):
            values = jnp.concatenate(
                [read(field, g * group + c, pl.ds(azimuth_cells, rows)) for c in range(group)], axis=0
            )
            high, low = halves(values)
            columns = jnp.dot(
                jnp.concatenate([high, low], axis=1), pick_radial[...], preferred_element_type=F32
            ).reshape(group, rows, flames)
            picked.append(jnp.sum(columns * pick_row[...][None], axis=1))
        real, imag = picked
        cosines, sines = gain_cos[...], gain_sin[...]
        amounts = jnp.concatenate(
            [cosines * real - sines * imag, cosines * imag + sines * real], axis=0
        )
        high = amounts.astype(BF16).astype(F32)
        flame_send[step] = pack([high, amounts - high])
        copies = start(blocks(flame_send.at[step], flame_recv.at[step], flame_sems.at[step]))
        flame_recv[step, 0] = flame_send[step, 0]
        return copies

    def squeeze(recv):
        lanes = lax.broadcasted_iota(I32, (8, LANES), 1)
        tiles = []
        for first in range(0, n_sector, 4):
            b = [recv[first + i] for i in range(4)]
            tiles.append(jnp.where(lanes < 96, b[0], b[1]))
            tiles.append(jnp.where(lanes < 64, b[1], b[2]))
            tiles.append(jnp.where(lanes < 32, b[2], b[3]))
        return jnp.concatenate(tiles, axis=1)

    loads[8].wait()
    loads[9].wait()
    halo_copies = send_sides(field_a, 0)
    flame_copies = send_flames(field_a, 0)

    first_axial = axial == 0
    last_axial = axial == n_axial - 1
    for copy in sound_copies:
        copy.wait_recv()
    low_pad = pl.ds(0, azimuth_cells)
    high_pad = pl.ds(rows + azimuth_cells, azimuth_cells)
    sound[:, low_pad, :] = jnp.where(first_axial, 0.0, sound[:, low_pad, :])
    sound[:, high_pad, :] = jnp.where(last_axial, 0.0, sound[:, high_pad, :])
    tile = (azimuth_cells, radial_cells)
    azimuth = lax.broadcasted_iota(I32, tile, 0)
    radial = lax.broadcasted_iota(I32, tile, 1)

    def one_coef(a, _):
        here = pl.multiple_of(a * azimuth_cells, azimuth_cells)
        s = read(sound, pl.ds(here + azimuth_cells, azimuth_cells))
        k_alo = 0.5 * (s + read(sound, pl.ds(here, azimuth_cells)))
        k_ahi = 0.5 * (s + read(sound, pl.ds(here + 2 * azimuth_cells, azimuth_cells)))
        side_lo = jnp.broadcast_to(read(sound_side, 0, pl.ds(a, 1)), tile)
        side_hi = jnp.broadcast_to(read(sound_side, 1, pl.ds(a, 1)), tile)
        k_slo = 0.5 * (s + jnp.where(azimuth == 0, side_lo, pltpu.roll(s, 1, 0)))
        k_shi = 0.5 * (
            s + jnp.where(azimuth == azimuth_cells - 1, side_hi, pltpu.roll(s, azimuth_cells - 1, 0))
        )
        k_rlo = jnp.where(radial == 0, 0.0, 0.5 * (s + pltpu.roll(s, 1, 1)))
        k_rhi = jnp.where(
            radial == radial_cells - 1, 0.0, 0.5 * (s + pltpu.roll(s, radial_cells - 1, 1))
        )
        scale = RELAX / (k_alo + k_ahi + k_slo + k_shi + k_rlo + k_rhi)
        at = pl.ds(here, azimuth_cells)
        coef[0, at, :] = scale
        coef[1, at, :] = scale * k_alo
        coef[2, at, :] = scale * k_ahi
        k_slo = scale * k_slo
        k_shi = scale * k_shi
        coef[3, at, :] = jnp.where(azimuth == 0, 0.0, k_slo)
        coef[4, at, :] = jnp.where(azimuth == azimuth_cells - 1, 0.0, k_shi)
        coef[5, at, :] = scale * k_rlo
        coef[6, at, :] = scale * k_rhi
        write(edge, 0, pl.ds(a, 1), k_slo[0:1])
        write(edge, 1, pl.ds(a, 1), k_shi[azimuth_cells - 1 : azimuth_cells])
        return 0

    lax.fori_loop(0, axial_cells, one_coef, 0)

    loads[10].wait()
    loads[11].wait()
    omega_real = [omega[0, m] for m in range(modes)]
    omega_imag = [omega[1, m] for m in range(modes)]

    def base_rows(field, a):
        here = pl.multiple_of(a * azimuth_cells, azimuth_cells)
        at = pl.ds(here, azimuth_cells)
        mid = pl.ds(here + azimuth_cells, azimuth_cells)
        top = pl.ds(here + 2 * azimuth_cells, azimuth_cells)
        scale, k_alo, k_ahi, k_slo, k_shi, k_rlo, k_rhi = (coef[i, at, :] for i in range(7))
        for m in range(modes):
            real, imag = read(field, m, mid), read(field, modes + m, mid)
            for c, x, mass in (
                (m, real, omega_real[m] * real - omega_imag[m] * imag),
                (modes + m, imag, omega_real[m] * imag + omega_imag[m] * real),
            ):
                near = k_alo * read(field, c, at) + k_ahi * read(field, c, top)
                near = near + k_slo * pltpu.roll(x, 1, 0)
                near = near + k_shi * pltpu.roll(x, azimuth_cells - 1, 0)
                near = near + k_rlo * pltpu.roll(x, 1, 1)
                near = near + k_rhi * pltpu.roll(x, radial_cells - 1, 1)
                write(base, c, at, (1.0 - RELAX) * x + scale * (rhs[c, at, :] + mass) + near)

    def make_base(field, halo, step):
        lax.fori_loop(1, axial_cells - 1, lambda a, _: (base_rows(field, a), 0)[1], 0)
        for copy in halo:
            copy.wait_recv()
        for c in range(channels):
            field[c, :, low_pad, :] = jnp.where(first_axial, 0.0, field[c, :, low_pad, :])
            field[c, :, high_pad, :] = jnp.where(last_axial, 0.0, field[c, :, high_pad, :])
        base_rows(field, 0)
        base_rows(field, axial_cells - 1)
        for side, row in ((0, 0), (1, azimuth_cells - 1)):
            at = pl.ds(row, axial_cells, azimuth_cells)
            for c in range(channels):
                for i in range(tiles):
                    base[c, i, at, :] = (
                        base[c, i, at, :] + edge[side, i] * side_recv[step, side, c, i]
                    )

    make_base(field_a, halo_copies, 0)

    for copy in cell_copies:
        copy.wait_recv()
    cells = squeeze(cell_recv).astype(I32)
    put_row[...] = one_hot(
        lax.broadcasted_iota(I32, (rows, slots), 0) == jnp.broadcast_to(cells[0:1], (rows, slots))
    )
    put_radial[...] = one_hot(
        lax.broadcasted_iota(I32, (radial_cells, slots), 0)
        == jnp.broadcast_to(cells[1:2], (radial_cells, slots))
    ).T

    chunk = rows // 4

    def flame_parts(copies, step):
        for copy in copies:
            copy.wait_recv()
        return halves(squeeze(flame_recv.at[step]))

    def flame_total(parts, first):
        hot = put_row[first : first + chunk, :]
        left = jnp.concatenate(
            [hot * part[c : c + 1, :] for part in parts for c in range(channels)], axis=0
        )
        totals = jnp.dot(left, put_radial[...], preferred_element_type=F32)
        half = channels * chunk
        return totals[:half] + totals[half:]

    parts = flame_parts(flame_copies, 0)
    for first in range(0, rows, chunk):
        totals = flame_total(parts, first)
        scale = coef[0, first : first + chunk, :]
        for c in range(channels):
            write(
                field_b,
                c,
                pl.ds(first + azimuth_cells, chunk),
                read(base, c, pl.ds(first, chunk)) - scale * totals[c * chunk : (c + 1) * chunk],
            )

    halo_copies = send_sides(field_b, 1)
    flame_copies = send_flames(field_b, 1)
    make_base(field_b, halo_copies, 1)
    parts = flame_parts(flame_copies, 1)
    loads[12].wait()
    sens_copies = []
    stores = []
    for i, first in enumerate(range(0, rows, chunk)):
        totals = flame_total(parts, first)
        at = pl.ds(first, chunk)
        scale = coef[0, at, :]
        sens = jnp.zeros((chunk, radial_cells), F32)
        for c in range(channels):
            x = read(base, c, at) - scale * totals[c * chunk : (c + 1) * chunk]
            result[c, at, :] = x
            term = x * direct[c, at, :].astype(F32)
            sens = sens + term if c < modes else sens - term
        sens_own[at, :] = sens
        sens_copies += start(
            [
                pltpu.make_async_remote_copy(
                    src_ref=sens_own.at[at],
                    dst_ref=sens_other.at[at],
                    send_sem=sens_sems.at[0, i],
                    recv_sem=sens_sems.at[1, i],
                    device_id={"modes": 1 - my_modes},
                    device_id_type=MESH,
                )
            ]
        )
        store = pltpu.make_async_copy(result.at[:, at], adjoint_hbm.at[:, at], out_sem.at[i])
        store.start()
        stores.append(store)
    for i, first in enumerate(range(0, rows, chunk)):
        at = pl.ds(first, chunk)
        sens_copies[i].wait_recv()
        sens_other[at, :] = sens_own[at, :] + sens_other[at, :]
    store = pltpu.make_async_copy(sens_other, sens_hbm, out_sem.at[4])
    store.start()
    stores.append(store)
    for copy in sends:
        copy.wait_send()
    for store in stores:
        store.wait()


def local(
    n_sector,
    n_axial,
    rhs,
    adjoint_start,
    sound_sq,
    direct_mode,
    omega_sq,
    flame_gain,
    delay_phase,
    delay_bin,
    flame_cell,
    injector_sector,
    injector_cell,
):
    parts, modes, axial_cells, azimuth_cells, radial_cells = rhs.shape
    channels = parts * modes
    rows = axial_cells * azimuth_cells
    flames = flame_cell.shape[1]
    slots = n_sector * CAP
    block = (channels, rows, radial_cells)
    tiles = radial_cells // LANES
    padded = (channels, tiles, rows + 2 * azimuth_cells, LANES)
    side = (tiles, axial_cells, LANES)
    plane = (rows, radial_cells)
    dma = pltpu.SemaphoreType.DMA
    vmem = pltpu.VMEM
    scratch = [
        vmem(block, F32),
        vmem(padded, F32),
        vmem(padded, F32),
        vmem(padded[1:], F32),
        vmem(block, BF16),
        pltpu.SMEM((2, modes), F32),
        vmem((1, flames), F32),
        vmem(delay_phase.shape, F32),
        vmem((1, flames), I32),
        vmem((1, flames), I32),
        vmem((1, flames), I32),
        vmem((1, flames), I32),
        vmem(block, F32),
        vmem((channels, tiles, rows, LANES), F32),
        vmem((7,) + plane, F32),
        vmem((2,) + side, F32),
        vmem((2 * radial_cells, flames), BF16),
        vmem((rows, flames), F32),
        vmem((LANES, flames), BF16),
        vmem((n_sector, flames), F32),
        vmem((modes, flames), F32),
        vmem((modes, flames), F32),
        vmem((rows, slots), BF16),
        vmem((slots, radial_cells), BF16),
        vmem((2,) + side, F32),
        vmem((2,) + side, F32),
        vmem((ITERS, 2, channels) + side, F32),
        vmem((ITERS, 2, channels) + side, F32),
        vmem((n_sector, 8, LANES), F32),
        vmem((n_sector, 8, LANES), F32),
        vmem((ITERS, n_sector, 8, LANES), F32),
        vmem((ITERS, n_sector, 8, LANES), F32),
        vmem(plane, F32),
        vmem(plane, F32),
        dma((13,)),
        dma((5,)),
        dma((2, 4)),
        dma((ITERS, 2, 4)),
        dma((2, n_sector)),
        dma((ITERS, 2, n_sector)),
        dma((2, 4)),
    ]
    anywhere = pl.BlockSpec(memory_space=pl.ANY)
    adjoint, sensitivity = pl.pallas_call(
        functools.partial(
            kernel, n_sector, n_axial, (modes, axial_cells, azimuth_cells, radial_cells)
        ),
        out_shape=(jax.ShapeDtypeStruct(block, F32), jax.ShapeDtypeStruct(plane, F32)),
        in_specs=[anywhere] * 11,
        out_specs=(anywhere, anywhere),
        scratch_shapes=scratch,
        compiler_params=pltpu.CompilerParams(
            collective_id=0, has_side_effects=True, vmem_limit_bytes=40 * 1024 * 1024
        ),
        name="helmholtz_steps",
    )(
        rhs.reshape(block),
        adjoint_start.reshape(block),
        sound_sq.reshape(plane),
        direct_mode.reshape(block),
        omega_sq,
        flame_gain,
        delay_phase,
        delay_bin,
        flame_cell,
        injector_sector.reshape(1, flames),
        injector_cell,
    )
    return adjoint.reshape(rhs.shape), sensitivity.reshape(sound_sq.shape)


def solution(mesh):
    placed = (
        P(None, "modes", "axial", "sector", None),
        P(None, "modes", "axial", "sector", None),
        P("axial", "sector", None),
        P(None, "modes", "axial", "sector", None),
        P(None, "modes"),
        P("axial", "sector"),
        P("modes", None),
        P("axial", "sector"),
        P("axial", "sector"),
        P("axial", "sector", None),
        P("axial", "sector"),
    )
    return jax.shard_map(
        functools.partial(local, mesh.shape["sector"], mesh.shape["axial"]),
        mesh=mesh,
        in_specs=placed,
        out_specs=(P(None, "modes", "axial", "sector", None), P("axial", "sector", None)),
        check_vma=False,
    )
```

```python
import functools

import jax
import jax.numpy as jnp
from jax import lax
from jax.experimental import pallas as pl
from jax.experimental.pallas import tpu as pltpu
from jax.sharding import PartitionSpec as P

ITERS = 2
RELAX = 0.6
CAP = 96
LANES = 128
MESH = pl.DeviceIdType.MESH
BF16 = jnp.bfloat16
F32 = jnp.float32
I32 = jnp.int32


def one_hot(flags):
    return jnp.where(flags, 1.0, 0.0).astype(BF16)


def halves(values):
    high = values.astype(BF16)
    return high, (values - high.astype(F32)).astype(BF16)


def dot_nt(left, right):
    return lax.dot_general(
        left, right, (((1,), (1,)), ((), ())), preferred_element_type=F32
    )


def read(ref, *index):
    *lead, at = index
    tiles = ref.shape[len(lead)]
    return jnp.concatenate([ref[(*lead, i, at)] for i in range(tiles)], axis=-1)


def write(ref, *index_and_value):
    *lead, at, value = index_and_value
    for i in range(ref.shape[len(lead)]):
        ref[(*lead, i, at)] = value[..., i * LANES : (i + 1) * LANES]


def flip(sector, mask, n_sector):
    bit = 1
    other = sector
    while bit < n_sector:
        if mask & bit:
            other = other + bit * (1 - 2 * (sector // bit % 2))
        bit *= 2
    return other


def partner_order(n_sector):
    hops = {mask: (0, 1, 2, 1)[mask // 2 % 4] + mask // 8 for mask in range(n_sector)}
    return sorted(range(n_sector), key=lambda mask: (hops[mask], mask))


def kernel(
    n_sector,
    n_axial,
    shape,
    rhs_hbm,
    start_hbm,
    sound_hbm,
    direct_hbm,
    omega_hbm,
    gain_hbm,
    phase_hbm,
    bin_hbm,
    source_hbm,
    sector_hbm,
    target_hbm,
    adjoint,
    sensitivity,
    rhs,
    field_a,
    field_b,
    sound,
    direct,
    omega,
    gain,
    phase,
    bins,
    source,
    sector,
    target,
    base,
    scale,
    k_axial,
    k_rest,
    edge,
    pick_radial,
    pick_row,
    picked_start,
    lane_hot,
    block_hot,
    gain_cos,
    gain_sin,
    put_row,
    put_edge,
    put_radial,
    match,
    sound_send,
    sound_side,
    side_send,
    side_recv,
    end_send,
    cell_send,
    cell_recv,
    flame_send,
    flame_recv,
    sens_own,
    sens_other,
    in_sem,
    sound_sems,
    halo_sems,
    cell_sems,
    flame_sems,
    sens_sems,
):
    modes, axial_cells, azimuth_cells, radial_cells = shape
    channels = 2 * modes
    rows = axial_cells * azimuth_cells
    flames = gain.shape[1]
    tiles = radial_cells // LANES
    half_blocks = n_sector // 2
    half = half_blocks * CAP
    near, far = 0, 1
    axial = lax.axis_index("axial")
    my_sector = lax.axis_index("sector")
    my_modes = lax.axis_index("modes")
    up_axial = lax.rem(axial + 1, n_axial)
    down_axial = lax.rem(axial + n_axial - 1, n_axial)
    next_sector = lax.rem(my_sector + 1, n_sector)
    last_sector = lax.rem(my_sector + n_sector - 1, n_sector)
    partners = [flip(my_sector, mask, n_sector) for mask in partner_order(n_sector)]

    barrier = pltpu.get_barrier_semaphore()
    for other in partners[1:]:
        pl.semaphore_signal(barrier, inc=1, device_id={"sector": other}, device_id_type=MESH)
    for other in (next_sector, last_sector):
        pl.semaphore_signal(barrier, inc=1, device_id={"sector": other}, device_id_type=MESH)
    for other in (up_axial, down_axial):
        pl.semaphore_signal(barrier, inc=1, device_id={"axial": other}, device_id_type=MESH)
    pl.semaphore_signal(
        barrier, inc=1, device_id={"modes": 1 - my_modes}, device_id_type=MESH
    )

    inner = pl.ds(azimuth_cells, rows)
    pieces = [pl.ds(i * LANES, LANES) for i in range(tiles)]
    loads = {}
    for name, source_ref, target_ref in (
        [("sector", sector_hbm, sector), ("target", target_hbm, target), ("source", source_hbm, source)]
        + [(("start", i), start_hbm.at[:, :, pieces[i]], field_a.at[:, i, inner]) for i in range(tiles)]
        + [(("sound", i), sound_hbm.at[:, pieces[i]], sound.at[i, inner]) for i in range(tiles)]
        + [("bins", bin_hbm, bins), ("phase", phase_hbm, phase), ("gain", gain_hbm, gain)]
        + [("omega", omega_hbm, omega), ("rhs", rhs_hbm, rhs), ("direct", direct_hbm, direct)]
    ):
        loads[name] = pltpu.make_async_copy(source_ref, target_ref, in_sem.at[len(loads)])
        if name not in ("rhs", "direct"):
            loads[name].start()

    def loaded(*names):
        for name in names:
            loads[name].wait()

    loaded("sector", "target", "source")
    partner = jnp.zeros((n_sector, LANES), I32)
    position = lax.broadcasted_iota(I32, (n_sector, LANES), 0)
    for p, other in enumerate(partners):
        partner = jnp.where(position == p, other, partner)
    partner = jnp.concatenate([partner] * (flames // LANES), axis=1)
    in_block = jnp.where(jnp.broadcast_to(sector[...], (n_sector, flames)) == partner, 1.0, 0.0)
    block_hot[...] = in_block
    before = one_hot(
        lax.broadcasted_iota(I32, (flames, flames), 0)
        < lax.broadcasted_iota(I32, (flames, flames), 1)
    )
    earlier = jnp.dot(in_block.astype(BF16), before, preferred_element_type=F32)
    rank = jnp.sum(in_block * earlier, axis=0, keepdims=True).astype(I32)
    block_of = jnp.sum(
        in_block * lax.broadcasted_iota(I32, (n_sector, flames), 0).astype(F32),
        axis=0,
        keepdims=True,
    ).astype(I32)
    lane = (rank + CAP * block_of) & (LANES - 1)
    lane_hot[...] = one_hot(
        lax.broadcasted_iota(I32, (LANES, flames), 0) == jnp.broadcast_to(lane, (LANES, flames))
    )

    def pack(parts):
        left = jnp.concatenate(
            [
                jnp.concatenate(
                    [part * block_hot[p : p + 1, :] for p in range(n_sector)], axis=0
                ).astype(BF16)
                for part in parts
            ],
            axis=0,
        )
        packed = dot_nt(left, lane_hot[...])
        total = packed[: 8 * n_sector]
        for i in range(1, len(parts)):
            total = total + packed[8 * n_sector * i : 8 * n_sector * (i + 1)]
        return total.reshape(n_sector, 8, LANES)

    target_row = (target[...] // radial_cells).astype(F32)
    target_radial = (target[...] % radial_cells).astype(F32)
    sub = lax.broadcasted_iota(I32, (8, flames), 0)
    cell_send[...] = pack(
        [
            jnp.where(
                sub == 0,
                jnp.broadcast_to(target_row, (8, flames)),
                jnp.where(sub == 1, jnp.broadcast_to(target_radial, (8, flames)), 0.0),
            )
        ]
    )

    def remote(src, dst, sems, i, device):
        return pltpu.make_async_remote_copy(
            src_ref=src,
            dst_ref=dst,
            send_sem=sems.at[0, i],
            recv_sem=sems.at[1, i],
            device_id=device,
            device_id_type=MESH,
        )

    low_pad = pl.ds(0, azimuth_cells)
    high_pad = pl.ds(rows + azimuth_cells, azimuth_cells)
    first_rows = pl.ds(azimuth_cells, azimuth_cells)
    last_rows = pl.ds(rows, azimuth_cells)

    def side_halo(send, recv, sems):
        return [
            remote(send.at[1], recv.at[0], sems, 2, {"sector": next_sector}),
            remote(send.at[0], recv.at[1], sems, 3, {"sector": last_sector}),
        ]

    def blocks(send, recv, sems):
        return [
            remote(send.at[p], recv.at[p], sems, p, {"sector": partners[p]})
            for p in reversed(range(1, n_sector))
        ]

    sends = []

    def start(copies):
        for copy in copies:
            copy.start()
        sends.extend(copies)
        return copies

    def received(copies):
        for copy in copies:
            copy.wait_recv()

    side_rows = [
        pl.ds(row, axial_cells, azimuth_cells) for row in (0, azimuth_cells - 1)
    ]
    padded_side_rows = [
        pl.ds(azimuth_cells + row, axial_cells, azimuth_cells) for row in (0, azimuth_cells - 1)
    ]

    loaded(*[("sound", i) for i in range(tiles)])
    for side in range(2):
        for i in range(tiles):
            sound_send[side, i] = sound[i, padded_side_rows[side], :]
    loaded(*[("start", i) for i in range(tiles)])
    loads["rhs"].start()
    for side in range(2):
        for c in range(channels):
            for i in range(tiles):
                side_send[0, side, c, i] = field_a[c, i, padded_side_rows[side], :]

    pl.semaphore_wait(barrier, n_sector + 4)

    cell_copies = start(blocks(cell_send, cell_recv, cell_sems))
    sound_copies = start(
        [
            remote(sound.at[:, last_rows], sound.at[:, low_pad], sound_sems, 0, {"axial": up_axial}),
            remote(sound.at[:, first_rows], sound.at[:, high_pad], sound_sems, 1, {"axial": down_axial}),
        ]
        + side_halo(sound_send, sound_side, sound_sems)
    )
    cell_recv[0] = cell_send[0]
    sems = halo_sems.at[0]
    halo_copies = start(
        side_halo(side_send.at[0], side_recv.at[0], sems)
        + [
            remote(field_a.at[:, :, last_rows], field_a.at[:, :, low_pad], sems, 0, {"axial": up_axial}),
            remote(field_a.at[:, :, first_rows], field_a.at[:, :, high_pad], sems, 1, {"axial": down_axial}),
        ]
    )

    cell = source[...]
    row_of = jnp.broadcast_to(cell // radial_cells, (rows, flames))
    pick_row[...] = jnp.where(lax.broadcasted_iota(I32, (rows, flames), 0) == row_of, 1.0, 0.0)
    radial_of = jnp.broadcast_to(cell % radial_cells, (radial_cells, flames))
    radial_hot = one_hot(lax.broadcasted_iota(I32, (radial_cells, flames), 0) == radial_of)
    pick_radial[:radial_cells] = radial_hot
    pick_radial[radial_cells:] = radial_hot

    loaded("bins", "phase", "gain")
    bin_count = phase.shape[1]
    bin_hot = jnp.where(
        lax.broadcasted_iota(I32, (bin_count, flames), 0)
        == jnp.broadcast_to(bins[...], (bin_count, flames)),
        1.0,
        0.0,
    )
    angle = phase[...]
    gains = jnp.broadcast_to(gain[...], (modes, flames))
    exact = lax.Precision.HIGHEST
    gain_cos[...] = gains * jnp.dot(
        jnp.cos(angle), bin_hot, precision=exact, preferred_element_type=F32
    )
    gain_sin[...] = -gains * jnp.dot(
        jnp.sin(angle), bin_hot, precision=exact, preferred_element_type=F32
    )

    def pick(planes):
        high, low = halves(jnp.concatenate(planes, axis=0))
        columns = jnp.dot(
            jnp.concatenate([high, low], axis=1), pick_radial[...], preferred_element_type=F32
        ).reshape(len(planes), rows, flames)
        return jnp.sum(columns * pick_row[...][None], axis=1)

    def pick_field(ref, at):
        return jnp.concatenate(
            [
                pick([read(ref, g * modes + m, at) for m in range(modes)])
                for g in range(2)
            ],
            axis=0,
        )

    def send_flames(picked, step):
        real, imag = picked[:modes], picked[modes:]
        cosines, sines = gain_cos[...], gain_sin[...]
        amounts = jnp.concatenate(
            [cosines * real - sines * imag, cosines * imag + sines * real], axis=0
        )
        high = amounts.astype(BF16).astype(F32)
        flame_send[step] = pack([high, amounts - high])
        copies = start(blocks(flame_send.at[step], flame_recv.at[step], flame_sems.at[step]))
        flame_recv[step, 0] = flame_send[step, 0]
        return copies[half_blocks:], copies[:half_blocks]

    picked_start[...] = pick_field(field_a, inner)
    near_copies, far_copies = send_flames(picked_start[...], 0)

    tile = (azimuth_cells, radial_cells)
    azimuth = lax.broadcasted_iota(I32, tile, 0)
    radial = lax.broadcasted_iota(I32, tile, 1)

    def own_rows(a):
        return pl.ds(pl.multiple_of(a * azimuth_cells, azimuth_cells), azimuth_cells)

    def couplings(a, _):
        s = read(sound, own_rows(a + 1))
        at = own_rows(a)
        k_rest[0, at, :] = jnp.where(azimuth == 0, 0.0, 0.5 * (s + pltpu.roll(s, 1, 0)))
        k_rest[1, at, :] = jnp.where(
            azimuth == azimuth_cells - 1, 0.0, 0.5 * (s + pltpu.roll(s, azimuth_cells - 1, 0))
        )
        k_rest[2, at, :] = jnp.where(radial == 0, 0.0, 0.5 * (s + pltpu.roll(s, 1, 1)))
        k_rest[3, at, :] = jnp.where(
            radial == radial_cells - 1, 0.0, 0.5 * (s + pltpu.roll(s, radial_cells - 1, 1))
        )
        return 0

    def axial_coupling(a, _):
        k_axial[own_rows(a), :] = 0.5 * (read(sound, own_rows(a)) + read(sound, own_rows(a + 1)))
        return 0

    lax.fori_loop(0, axial_cells, couplings, 0)
    lax.fori_loop(1, axial_cells, axial_coupling, 0)

    loaded("omega", "rhs")
    loads["direct"].start()
    omega_real = [omega[0, m] for m in range(modes)]
    omega_imag = [omega[1, m] for m in range(modes)]

    def base_rows(field, a, low, high):
        at, mid, top = own_rows(a), own_rows(a + 1), own_rows(a + 2)
        k_slo, k_shi, k_rlo, k_rhi = (k_rest[i, at, :] for i in range(4))
        k_alo = k_axial[at, :] if low else None
        k_ahi = k_axial[mid, :] if high else None
        for m in range(modes):
            real, imag = read(field, m, mid), read(field, modes + m, mid)
            for c, x, mass in (
                (m, real, omega_real[m] * real - omega_imag[m] * imag),
                (modes + m, imag, omega_real[m] * imag + omega_imag[m] * real),
            ):
                total = rhs[c, at, :] + mass
                if low:
                    total = total + k_alo * read(field, c, at)
                if high:
                    total = total + k_ahi * read(field, c, top)
                total = total + k_slo * pltpu.roll(x, 1, 0)
                total = total + k_shi * pltpu.roll(x, azimuth_cells - 1, 0)
                total = total + k_rlo * pltpu.roll(x, 1, 1)
                total = total + k_rhi * pltpu.roll(x, radial_cells - 1, 1)
                write(base, c, at, total)

    def make_base(field):
        lax.fori_loop(
            1, axial_cells - 1, lambda a, _: (base_rows(field, a, True, True), 0)[1], 0
        )
        base_rows(field, 0, False, True)
        base_rows(field, axial_cells - 1, True, False)

    first_axial = axial == 0
    last_axial = axial == n_axial - 1
    first, last = pl.ds(0, azimuth_cells), pl.ds(rows - azimuth_cells, azimuth_cells)

    def add_halo(field, step):
        k_low = k_axial[pl.ds(0, azimuth_cells), :]
        k_high = k_axial[pl.ds(rows, azimuth_cells), :]
        for c in range(channels):
            below = jnp.where(first_axial, 0.0, read(field, c, low_pad))
            write(base, c, first, read(base, c, first) + k_low * below)
            above = jnp.where(last_axial, 0.0, read(field, c, high_pad))
            write(base, c, last, read(base, c, last) + k_high * above)
        for side in range(2):
            at = side_rows[side]
            for c in range(channels):
                for i in range(tiles):
                    base[c, i, at, :] = (
                        base[c, i, at, :] + edge[side, i] * side_recv[step, side, c, i]
                    )

    make_base(field_a)

    def squeeze(recv, group):
        lanes = lax.broadcasted_iota(I32, (8, LANES), 1)
        parts = []
        for start_block in range(group * half_blocks, (group + 1) * half_blocks, 4):
            b = [recv[start_block + i] for i in range(4)]
            parts.append(jnp.where(lanes < 96, b[0], b[1]))
            parts.append(jnp.where(lanes < 64, b[1], b[2]))
            parts.append(jnp.where(lanes < 32, b[2], b[3]))
        return jnp.concatenate(parts, axis=1)

    def put_hots(group):
        cells = squeeze(cell_recv, group)
        row, column = cells[0:1], cells[1:2]
        put_row[group] = one_hot(
            lax.broadcasted_iota(I32, (rows, half), 0).astype(F32)
            == jnp.broadcast_to(row, (rows, half))
        )
        upright = jnp.broadcast_to(column, (LANES, half)).T
        put_radial[group] = one_hot(
            jnp.concatenate([upright] * tiles, axis=1)
            == lax.broadcasted_iota(I32, (half, radial_cells), 1).astype(F32)
        )
        return row, column

    def add_flames(parts, hot, group):
        left = jnp.concatenate(
            [hot * part[c : c + 1, :] for part in parts for c in range(channels)], axis=0
        )
        totals = jnp.dot(left, put_radial[group], preferred_element_type=F32)
        middle = totals.shape[0] // 2
        return totals[:middle] + totals[middle:]

    chunk = rows // 4

    def subtract_near(step):
        parts = halves(squeeze(flame_recv.at[step], near))
        for top in range(0, rows, chunk):
            at = pl.ds(top, chunk)
            totals = add_flames(parts, put_row[near, top : top + chunk, :], near)
            for c in range(channels):
                write(base, c, at, read(base, c, at) - totals[c * chunk : (c + 1) * chunk])

    received(cell_copies[half_blocks:])
    put_hots(near)
    received(near_copies)
    subtract_near(0)

    received(sound_copies)
    k_axial[first, :] = 0.5 * (
        read(sound, first_rows) + jnp.where(first_axial, 0.0, read(sound, low_pad))
    )
    k_axial[pl.ds(rows, azimuth_cells), :] = 0.5 * (
        read(sound, last_rows) + jnp.where(last_axial, 0.0, read(sound, high_pad))
    )
    for side in range(2):
        for i in range(tiles):
            edge[side, i] = 0.5 * (sound[i, padded_side_rows[side], :] + sound_side[side, i])

    def scales(a, _):
        at = own_rows(a)
        low = jnp.broadcast_to(read(edge, 0, pl.ds(a, 1)), tile)
        high = jnp.broadcast_to(read(edge, 1, pl.ds(a, 1)), tile)
        weights = k_axial[at, :] + k_axial[own_rows(a + 1), :] + k_rest[2, at, :] + k_rest[3, at, :]
        weights = weights + jnp.where(azimuth == 0, low, k_rest[0, at, :])
        weights = weights + jnp.where(azimuth == azimuth_cells - 1, high, k_rest[1, at, :])
        write(scale, at, RELAX / weights)
        return 0

    lax.fori_loop(0, axial_cells, scales, 0)
    all_rows = pl.ds(0, rows)
    picked_scale = pick([read(scale, all_rows)])

    received(cell_copies[:half_blocks])
    row, column = put_hots(far)
    edge_rows = 2 * axial_cells + 2 * azimuth_cells
    i = lax.broadcasted_iota(I32, (edge_rows, half), 0)
    edge_row = jnp.where(
        i < axial_cells,
        i * azimuth_cells,
        jnp.where(
            i < 2 * axial_cells,
            (i - axial_cells) * azimuth_cells + azimuth_cells - 1,
            jnp.where(
                i < 2 * axial_cells + azimuth_cells,
                i - 2 * axial_cells,
                i - 2 * axial_cells - 2 * azimuth_cells + rows,
            ),
        ),
    )
    put_edge[...] = one_hot(edge_row.astype(F32) == jnp.broadcast_to(row, (edge_rows, half)))
    upright = jnp.broadcast_to(row * radial_cells + column, (LANES, half)).T
    match[...] = one_hot(
        jnp.concatenate([upright] * (flames // LANES), axis=1)
        == jnp.broadcast_to(cell.astype(F32), (half, flames))
    )

    received(halo_copies)
    add_halo(field_a, 0)
    picked_base = pick_field(base, all_rows)

    received(far_copies)
    parts = halves(squeeze(flame_recv.at[0], far))
    found = jnp.dot(jnp.concatenate(parts, axis=0), match[...], preferred_element_type=F32)
    found = found[:channels] + found[channels:]
    picked = (1.0 - RELAX) * picked_start[...] + picked_scale * (picked_base - found)
    near_copies, far_copies = send_flames(picked, 1)

    totals = add_flames(parts, put_edge[...], far)
    for c in range(channels):
        here = c * edge_rows
        for side in range(2):
            for i in range(tiles):
                added = totals[
                    here + side * axial_cells : here + (side + 1) * axial_cells,
                    i * LANES : (i + 1) * LANES,
                ]
                side_send[1, side, c, i] = (1.0 - RELAX) * side_send[0, side, c, i] + scale[
                    i, side_rows[side], :
                ] * (base[c, i, side_rows[side], :] - added)
        here = here + 2 * axial_cells
        for end, at, padded_at in ((0, first, first_rows), (1, last, last_rows)):
            added = totals[here + end * azimuth_cells : here + (end + 1) * azimuth_cells]
            write(
                end_send,
                end,
                c,
                pl.ds(0, azimuth_cells),
                (1.0 - RELAX) * read(field_a, c, padded_at)
                + read(scale, at) * (read(base, c, at) - added),
            )
    sems = halo_sems.at[1]
    halo_copies = start(
        side_halo(side_send.at[1], side_recv.at[1], sems)
        + [
            remote(end_send.at[1], field_b.at[:, :, low_pad], sems, 0, {"axial": up_axial}),
            remote(end_send.at[0], field_b.at[:, :, high_pad], sems, 1, {"axial": down_axial}),
        ]
    )

    for top in range(0, rows, chunk):
        totals = add_flames(parts, put_row[far, top : top + chunk, :], far)
        at = pl.ds(top, chunk)
        padded_at = pl.ds(top + azimuth_cells, chunk)
        for c in range(channels):
            write(
                field_b,
                c,
                padded_at,
                (1.0 - RELAX) * read(field_a, c, padded_at)
                + read(scale, at) * (read(base, c, at) - totals[c * chunk : (c + 1) * chunk]),
            )

    make_base(field_b)
    received(near_copies)
    subtract_near(1)
    received(halo_copies)
    add_halo(field_b, 1)
    loaded("direct")
    received(far_copies)
    parts = halves(squeeze(flame_recv.at[1], far))
    sens_copies = []
    for number, top in enumerate(range(0, rows, chunk)):
        totals = add_flames(parts, put_row[far, top : top + chunk, :], far)
        at = pl.ds(top, chunk)
        padded_at = pl.ds(top + azimuth_cells, chunk)
        sens = jnp.zeros((chunk, radial_cells), F32)
        for c in range(channels):
            x = (1.0 - RELAX) * read(field_b, c, padded_at) + read(scale, at) * (
                read(base, c, at) - totals[c * chunk : (c + 1) * chunk]
            )
            adjoint[c, at, :] = x
            term = x * direct[c, at, :].astype(F32)
            sens = sens + term if c < modes else sens - term
        sens_own[at, :] = sens
        sens_copies += start(
            [remote(sens_own.at[at], sens_other.at[at], sens_sems, number, {"modes": 1 - my_modes})]
        )
    for number, top in enumerate(range(0, rows, chunk)):
        at = pl.ds(top, chunk)
        received([sens_copies[number]])
        sensitivity[at, :] = sens_own[at, :] + sens_other[at, :]
    for copy in sends:
        copy.wait_send()


def local(
    n_sector,
    n_axial,
    rhs,
    adjoint_start,
    sound_sq,
    direct_mode,
    omega_sq,
    flame_gain,
    delay_phase,
    delay_bin,
    flame_cell,
    injector_sector,
    injector_cell,
):
    parts, modes, axial_cells, azimuth_cells, radial_cells = rhs.shape
    channels = parts * modes
    rows = axial_cells * azimuth_cells
    flames = flame_cell.shape[1]
    half = n_sector // 2 * CAP
    tiles = radial_cells // LANES
    block = (channels, rows, radial_cells)
    padded = (channels, tiles, rows + 2 * azimuth_cells, LANES)
    side = (tiles, axial_cells, LANES)
    plane = (rows, radial_cells)
    dma = pltpu.SemaphoreType.DMA
    vmem = pltpu.VMEM
    scratch = [
        vmem(block, F32),
        vmem(padded, F32),
        vmem(padded, F32),
        vmem(padded[1:], F32),
        vmem(block, BF16),
        pltpu.SMEM((2, modes), F32),
        vmem((1, flames), F32),
        vmem(delay_phase.shape, F32),
        vmem((1, flames), I32),
        vmem((1, flames), I32),
        vmem((1, flames), I32),
        vmem((1, flames), I32),
        vmem((channels, tiles, rows, LANES), F32),
        vmem((tiles, rows, LANES), F32),
        vmem((rows + azimuth_cells, radial_cells), F32),
        vmem((4,) + plane, F32),
        vmem((2,) + side, F32),
        vmem((2 * radial_cells, flames), BF16),
        vmem((rows, flames), F32),
        vmem((channels, flames), F32),
        vmem((LANES, flames), BF16),
        vmem((n_sector, flames), F32),
        vmem((modes, flames), F32),
        vmem((modes, flames), F32),
        vmem((2, rows, half), BF16),
        vmem((2 * (axial_cells + azimuth_cells), half), BF16),
        vmem((2, half, radial_cells), BF16),
        vmem((half, flames), BF16),
        vmem((2,) + side, F32),
        vmem((2,) + side, F32),
        vmem((ITERS, 2, channels) + side, F32),
        vmem((ITERS, 2, channels) + side, F32),
        vmem((2, channels, tiles, azimuth_cells, LANES), F32),
        vmem((n_sector, 8, LANES), F32),
        vmem((n_sector, 8, LANES), F32),
        vmem((ITERS, n_sector, 8, LANES), F32),
        vmem((ITERS, n_sector, 8, LANES), F32),
        vmem(plane, F32),
        vmem(plane, F32),
        dma((9 + 2 * tiles,)),
        dma((2, 4)),
        dma((ITERS, 2, 4)),
        dma((2, n_sector)),
        dma((ITERS, 2, n_sector)),
        dma((2, 4)),
    ]
    in_hbm = pl.BlockSpec(memory_space=pltpu.HBM)

    def stay(array):
        return pltpu.with_memory_space_constraint(array, pltpu.HBM)

    in_vmem = pl.BlockSpec(memory_space=pltpu.VMEM)
    adjoint, sensitivity = pl.pallas_call(
        functools.partial(
            kernel, n_sector, n_axial, (modes, axial_cells, azimuth_cells, radial_cells)
        ),
        out_shape=(jax.ShapeDtypeStruct(block, F32), jax.ShapeDtypeStruct(plane, F32)),
        in_specs=[in_hbm] * 11,
        out_specs=(in_vmem, in_vmem),
        scratch_shapes=scratch,
        compiler_params=pltpu.CompilerParams(
            collective_id=0, has_side_effects=True, vmem_limit_bytes=40 * 1024 * 1024
        ),
        name="helmholtz_steps",
    )(
        stay(rhs.reshape(block)),
        stay(adjoint_start.reshape(block)),
        stay(sound_sq.reshape(plane)),
        stay(direct_mode.reshape(block)),
        stay(omega_sq),
        stay(flame_gain),
        stay(delay_phase),
        stay(delay_bin),
        stay(flame_cell),
        stay(injector_sector.reshape(1, flames)),
        stay(injector_cell),
    )
    return adjoint.reshape(rhs.shape), sensitivity.reshape(sound_sq.shape)


def solution(mesh):
    placed = (
        P(None, "modes", "axial", "sector", None),
        P(None, "modes", "axial", "sector", None),
        P("axial", "sector", None),
        P(None, "modes", "axial", "sector", None),
        P(None, "modes"),
        P("axial", "sector"),
        P("modes", None),
        P("axial", "sector"),
        P("axial", "sector"),
        P("axial", "sector", None),
        P("axial", "sector"),
    )
    return jax.shard_map(
        functools.partial(local, mesh.shape["sector"], mesh.shape["axial"]),
        mesh=mesh,
        in_specs=placed,
        out_specs=(P(None, "modes", "axial", "sector", None), P("axial", "sector", None)),
        check_vma=False,
    )
```

```python
import functools

import jax
import jax.numpy as jnp
from jax import lax
from jax.experimental import pallas as pl
from jax.experimental.pallas import tpu as pltpu
from jax.sharding import PartitionSpec as P

ITERS = 2
RELAX = 0.6
CAP = 96
LANES = 128
MESH = pl.DeviceIdType.MESH
BF16 = jnp.bfloat16
F32 = jnp.float32
I32 = jnp.int32


def one_hot(flags):
    return jnp.where(flags, 1.0, 0.0).astype(BF16)


def halves(values):
    high = values.astype(BF16)
    return high, (values - high.astype(F32)).astype(BF16)


def dot_nt(left, right):
    return lax.dot_general(
        left, right, (((1,), (1,)), ((), ())), preferred_element_type=F32
    )


def read(ref, *index):
    *lead, at = index
    tiles = ref.shape[len(lead)]
    return jnp.concatenate([ref[(*lead, i, at)] for i in range(tiles)], axis=-1)


def write(ref, *index_and_value):
    *lead, at, value = index_and_value
    for i in range(ref.shape[len(lead)]):
        ref[(*lead, i, at)] = value[..., i * LANES : (i + 1) * LANES]


def flip(sector, mask, n_sector):
    bit = 1
    other = sector
    while bit < n_sector:
        if mask & bit:
            other = other + bit * (1 - 2 * (sector // bit % 2))
        bit *= 2
    return other


def partner_order(n_sector):
    hops = {mask: (0, 1, 2, 1)[mask // 2 % 4] + mask // 8 for mask in range(n_sector)}
    return sorted(range(n_sector), key=lambda mask: (hops[mask], mask))


def kernel(
    n_sector,
    n_axial,
    shape,
    rhs_hbm,
    start_hbm,
    sound_hbm,
    direct_hbm,
    omega_hbm,
    gain_hbm,
    phase_hbm,
    bin_hbm,
    source_hbm,
    sector_hbm,
    target_hbm,
    adjoint,
    sensitivity,
    rhs,
    field_a,
    field_b,
    sound,
    direct,
    omega,
    gain,
    phase,
    bins,
    source,
    sector,
    target,
    base,
    scale,
    k_axial,
    k_rest,
    edge,
    pick_radial,
    pick_row,
    picked_start,
    lane_hot,
    block_hot,
    gain_cos,
    gain_sin,
    put_row,
    put_edge,
    put_radial,
    match,
    sound_send,
    sound_side,
    side_send,
    side_recv,
    end_send,
    end_recv,
    sound_end,
    cell_send,
    cell_recv,
    flame_send,
    flame_recv,
    direct_tiles,
    slot_direct,
    sens_own,
    sens_other,
    sens_sum,
    edge_own,
    edge_other,
    slot_own,
    slot_other,
    in_sem,
    sound_sems,
    halo_sems,
    cell_sems,
    flame_sems,
    sens_sems,
):
    modes, axial_cells, azimuth_cells, radial_cells = shape
    channels = 2 * modes
    rows = axial_cells * azimuth_cells
    flames = gain.shape[1]
    tiles = radial_cells // LANES
    half_blocks = n_sector // 2
    half = half_blocks * CAP
    near, far = 0, 1
    axial = lax.axis_index("axial")
    my_sector = lax.axis_index("sector")
    my_modes = lax.axis_index("modes")
    up_axial = lax.rem(axial + 1, n_axial)
    down_axial = lax.rem(axial + n_axial - 1, n_axial)
    next_sector = lax.rem(my_sector + 1, n_sector)
    last_sector = lax.rem(my_sector + n_sector - 1, n_sector)
    partners = [flip(my_sector, mask, n_sector) for mask in partner_order(n_sector)]

    barrier = pltpu.get_barrier_semaphore()
    for other in partners[1:]:
        pl.semaphore_signal(barrier, inc=1, device_id={"sector": other}, device_id_type=MESH)
    for other in (next_sector, last_sector):
        pl.semaphore_signal(barrier, inc=1, device_id={"sector": other}, device_id_type=MESH)
    for other in (up_axial, down_axial):
        pl.semaphore_signal(barrier, inc=1, device_id={"axial": other}, device_id_type=MESH)
    pl.semaphore_signal(
        barrier, inc=1, device_id={"modes": 1 - my_modes}, device_id_type=MESH
    )

    inner = pl.ds(azimuth_cells, rows)
    pieces = [pl.ds(i * LANES, LANES) for i in range(tiles)]
    loads = {}
    for name, source_ref, target_ref in (
        [("sector", sector_hbm, sector), ("target", target_hbm, target), ("source", source_hbm, source)]
        + [("bins", bin_hbm, bins), ("phase", phase_hbm, phase), ("gain", gain_hbm, gain)]
        + [(("sound", i), sound_hbm.at[:, pieces[i]], sound.at[i, inner]) for i in range(tiles)]
        + [(("start", i), start_hbm.at[:, :, pieces[i]], field_a.at[:, i, inner]) for i in range(tiles)]
        + [("omega", omega_hbm, omega), ("rhs", rhs_hbm, rhs), ("direct", direct_hbm, direct)]
    ):
        loads[name] = pltpu.make_async_copy(source_ref, target_ref, in_sem.at[len(loads)])
        if name not in ("rhs", "direct"):
            loads[name].start()

    def loaded(*names):
        for name in names:
            loads[name].wait()

    loaded("sector", "target", "source")
    partner = jnp.zeros((n_sector, LANES), I32)
    position = lax.broadcasted_iota(I32, (n_sector, LANES), 0)
    for p, other in enumerate(partners):
        partner = jnp.where(position == p, other, partner)
    partner = jnp.concatenate([partner] * (flames // LANES), axis=1)
    in_block = jnp.where(jnp.broadcast_to(sector[...], (n_sector, flames)) == partner, 1.0, 0.0)
    block_hot[...] = in_block
    before = one_hot(
        lax.broadcasted_iota(I32, (flames, flames), 0)
        < lax.broadcasted_iota(I32, (flames, flames), 1)
    )
    earlier = jnp.dot(in_block.astype(BF16), before, preferred_element_type=F32)
    rank = jnp.sum(in_block * earlier, axis=0, keepdims=True).astype(I32)
    block_of = jnp.sum(
        in_block * lax.broadcasted_iota(I32, (n_sector, flames), 0).astype(F32),
        axis=0,
        keepdims=True,
    ).astype(I32)
    lane = (rank + CAP * block_of) & (LANES - 1)
    lane_hot[...] = one_hot(
        lax.broadcasted_iota(I32, (LANES, flames), 0) == jnp.broadcast_to(lane, (LANES, flames))
    )

    def pack(parts):
        left = jnp.concatenate(
            [
                jnp.concatenate(
                    [part * block_hot[p : p + 1, :] for p in range(n_sector)], axis=0
                ).astype(BF16)
                for part in parts
            ],
            axis=0,
        )
        packed = dot_nt(left, lane_hot[...])
        total = packed[: 8 * n_sector]
        for i in range(1, len(parts)):
            total = total + packed[8 * n_sector * i : 8 * n_sector * (i + 1)]
        return total.reshape(n_sector, 8, LANES)

    target_row = (target[...] // radial_cells).astype(F32)
    target_radial = (target[...] % radial_cells).astype(F32)
    sub = lax.broadcasted_iota(I32, (8, flames), 0)
    cell_send[...] = pack(
        [
            jnp.where(
                sub == 0,
                jnp.broadcast_to(target_row, (8, flames)),
                jnp.where(sub == 1, jnp.broadcast_to(target_radial, (8, flames)), 0.0),
            )
        ]
    )

    def remote(src, dst, send_sem, recv_sem, device):
        return pltpu.make_async_remote_copy(
            src_ref=src,
            dst_ref=dst,
            send_sem=send_sem,
            recv_sem=recv_sem,
            device_id=device,
            device_id_type=MESH,
        )

    def wait_bytes(ref, sem):
        pltpu.make_async_copy(ref, ref, sem).wait()

    first_rows = pl.ds(azimuth_cells, azimuth_cells)
    last_rows = pl.ds(rows, azimuth_cells)
    sent = []

    def start_sides(send, recv, sems):
        remote(send.at[1], recv.at[0], sems.at[0, 0], sems.at[1, 0], {"sector": next_sector}).start()
        remote(send.at[0], recv.at[1], sems.at[0, 0], sems.at[1, 0], {"sector": last_sector}).start()
        sent.append((recv, sems.at[0, 0]))

    def start_ends(first, last, recv, sems):
        remote(last, recv.at[0], sems.at[0, 1], sems.at[1, 1], {"axial": up_axial}).start()
        remote(first, recv.at[1], sems.at[0, 1], sems.at[1, 1], {"axial": down_axial}).start()
        sent.append((recv, sems.at[0, 1]))

    def start_blocks(send, recv, sems):
        for p in reversed(range(1, n_sector)):
            group = 0 if p < half_blocks else 1
            remote(
                send.at[p], recv.at[p], sems.at[2], sems.at[group], {"sector": partners[p]}
            ).start()
        sent.append((send.at[pl.ds(1, n_sector - 1)], sems.at[2]))

    def wait_blocks(recv, sems, group):
        start = max(1, group * half_blocks)
        wait_bytes(recv.at[pl.ds(start, (group + 1) * half_blocks - start)], sems.at[group])

    def start_partner(send, recv, i):
        remote(
            send, recv, sens_sems.at[0, i], sens_sems.at[1, i], {"modes": 1 - my_modes}
        ).start()
        sent.append((send, sens_sems.at[0, i]))

    side_rows = [
        pl.ds(row, axial_cells, azimuth_cells) for row in (0, azimuth_cells - 1)
    ]
    padded_side_rows = [
        pl.ds(azimuth_cells + row, axial_cells, azimuth_cells) for row in (0, azimuth_cells - 1)
    ]

    cell = source[...]
    row_of = jnp.broadcast_to(cell // radial_cells, (rows, flames))
    pick_row[...] = jnp.where(lax.broadcasted_iota(I32, (rows, flames), 0) == row_of, 1.0, 0.0)
    radial_of = jnp.broadcast_to(cell % radial_cells, (radial_cells, flames))
    radial_hot = one_hot(lax.broadcasted_iota(I32, (radial_cells, flames), 0) == radial_of)
    pick_radial[:radial_cells] = radial_hot
    pick_radial[radial_cells:] = radial_hot

    loaded("bins", "phase", "gain")
    bin_count = phase.shape[1]
    bin_hot = jnp.where(
        lax.broadcasted_iota(I32, (bin_count, flames), 0)
        == jnp.broadcast_to(bins[...], (bin_count, flames)),
        1.0,
        0.0,
    )
    angle = phase[...]
    gains = jnp.broadcast_to(gain[...], (modes, flames))
    exact = lax.Precision.HIGHEST
    gain_cos[...] = gains * jnp.dot(
        jnp.cos(angle), bin_hot, precision=exact, preferred_element_type=F32
    )
    gain_sin[...] = -gains * jnp.dot(
        jnp.sin(angle), bin_hot, precision=exact, preferred_element_type=F32
    )

    loaded(*[("sound", i) for i in range(tiles)])
    for side in range(2):
        for i in range(tiles):
            sound_send[side, i] = sound[i, padded_side_rows[side], :]

    pl.semaphore_wait(barrier, n_sector + 4)

    start_blocks(cell_send, cell_recv, cell_sems)
    start_ends(sound.at[:, first_rows], sound.at[:, last_rows], sound_end, sound_sems)
    start_sides(sound_send, sound_side, sound_sems)
    cell_recv[0] = cell_send[0]

    loaded(*[("start", i) for i in range(tiles)])
    loads["rhs"].start()
    sems = halo_sems.at[0]
    start_ends(field_a.at[:, :, first_rows], field_a.at[:, :, last_rows], end_recv.at[0], sems)
    for side in range(2):
        for c in range(channels):
            for i in range(tiles):
                side_send[0, side, c, i] = field_a[c, i, padded_side_rows[side], :]
    start_sides(side_send.at[0], side_recv.at[0], sems)

    def pick(planes):
        high, low = halves(jnp.concatenate(planes, axis=0))
        columns = jnp.dot(
            jnp.concatenate([high, low], axis=1), pick_radial[...], preferred_element_type=F32
        ).reshape(len(planes), rows, flames)
        return jnp.sum(columns * pick_row[...][None], axis=1)

    def pick_field(ref, at):
        return jnp.concatenate(
            [
                pick([read(ref, g * modes + m, at) for m in range(modes)])
                for g in range(2)
            ],
            axis=0,
        )

    def send_flames(picked, step):
        real, imag = picked[:modes], picked[modes:]
        cosines, sines = gain_cos[...], gain_sin[...]
        amounts = jnp.concatenate(
            [cosines * real - sines * imag, cosines * imag + sines * real], axis=0
        )
        high = amounts.astype(BF16).astype(F32)
        flame_send[step] = pack([high, amounts - high])
        start_blocks(flame_send.at[step], flame_recv.at[step], flame_sems.at[step])
        flame_recv[step, 0] = flame_send[step, 0]

    picked_start[...] = pick_field(field_a, inner)
    send_flames(picked_start[...], 0)

    tile = (azimuth_cells, radial_cells)
    azimuth = lax.broadcasted_iota(I32, tile, 0)
    radial = lax.broadcasted_iota(I32, tile, 1)

    def own_rows(a):
        return pl.ds(pl.multiple_of(a * azimuth_cells, azimuth_cells), azimuth_cells)

    def couplings(a, _):
        s = read(sound, own_rows(a + 1))
        at = own_rows(a)
        k_rest[0, at, :] = jnp.where(azimuth == 0, 0.0, 0.5 * (s + pltpu.roll(s, 1, 0)))
        k_rest[1, at, :] = jnp.where(
            azimuth == azimuth_cells - 1, 0.0, 0.5 * (s + pltpu.roll(s, azimuth_cells - 1, 0))
        )
        k_rest[2, at, :] = jnp.where(radial == 0, 0.0, 0.5 * (s + pltpu.roll(s, 1, 1)))
        k_rest[3, at, :] = jnp.where(
            radial == radial_cells - 1, 0.0, 0.5 * (s + pltpu.roll(s, radial_cells - 1, 1))
        )
        return 0

    def axial_coupling(a, _):
        k_axial[own_rows(a), :] = 0.5 * (read(sound, own_rows(a)) + read(sound, own_rows(a + 1)))
        return 0

    lax.fori_loop(0, axial_cells, couplings, 0, unroll=True)
    lax.fori_loop(1, axial_cells, axial_coupling, 0, unroll=True)

    loaded("omega", "rhs")
    loads["direct"].start()
    omega_real = [omega[0, m] for m in range(modes)]
    omega_imag = [omega[1, m] for m in range(modes)]

    def base_rows(field, a, low, high):
        at, mid, top = own_rows(a), own_rows(a + 1), own_rows(a + 2)
        k_slo, k_shi, k_rlo, k_rhi = (k_rest[i, at, :] for i in range(4))
        k_alo = k_axial[at, :] if low else None
        k_ahi = k_axial[mid, :] if high else None
        for m in range(modes):
            real, imag = read(field, m, mid), read(field, modes + m, mid)
            for c, x, mass in (
                (m, real, omega_real[m] * real - omega_imag[m] * imag),
                (modes + m, imag, omega_real[m] * imag + omega_imag[m] * real),
            ):
                total = rhs[c, at, :] + mass
                if low:
                    total = total + k_alo * read(field, c, at)
                if high:
                    total = total + k_ahi * read(field, c, top)
                total = total + k_slo * pltpu.roll(x, 1, 0)
                total = total + k_shi * pltpu.roll(x, azimuth_cells - 1, 0)
                total = total + k_rlo * pltpu.roll(x, 1, 1)
                total = total + k_rhi * pltpu.roll(x, radial_cells - 1, 1)
                write(base, c, at, total)

    def make_base(field, low, high):
        for a in range(low, high):
            base_rows(field, a, a > 0, a < axial_cells - 1)

    first_axial = axial == 0
    last_axial = axial == n_axial - 1
    first, last = pl.ds(0, azimuth_cells), pl.ds(rows - azimuth_cells, azimuth_cells)
    whole = pl.ds(0, azimuth_cells)

    edge_rows = 2 * axial_cells + 2 * azimuth_cells

    def signed_sum(terms):
        return sum(terms[1:modes], terms[0]) - sum(terms[modes + 1 :], terms[modes])

    def add_halo(step):
        wait_bytes(end_recv.at[step], halo_sems.at[step, 1, 1])
        k_low = k_axial[pl.ds(0, azimuth_cells), :]
        k_high = k_axial[pl.ds(rows, azimuth_cells), :]
        low_terms, high_terms = [], []
        for c in range(channels):
            below = k_low * jnp.where(first_axial, 0.0, read(end_recv, step, 0, c, whole))
            above = k_high * jnp.where(last_axial, 0.0, read(end_recv, step, 1, c, whole))
            write(base, c, first, read(base, c, first) + below)
            write(base, c, last, read(base, c, last) + above)
            if step == ITERS - 1:
                low_terms.append(below * read(direct_tiles, c, first))
                high_terms.append(above * read(direct_tiles, c, last))
        wait_bytes(side_recv.at[step], halo_sems.at[step, 1, 0])
        for side in range(2):
            at = side_rows[side]
            for i in range(tiles):
                terms = []
                for c in range(channels):
                    added = edge[side, i] * side_recv[step, side, c, i]
                    base[c, i, at, :] = base[c, i, at, :] + added
                    if step == ITERS - 1:
                        terms.append(added * direct_tiles[c, i, at, :])
                if step == ITERS - 1:
                    edge_own[i, pl.ds(side * axial_cells, axial_cells), :] = scale[
                        i, at, :
                    ] * signed_sum(terms)
        if step == ITERS - 1:
            for end, at, terms in ((0, first, low_terms), (1, last, high_terms)):
                write(
                    edge_own,
                    pl.ds(2 * axial_cells + end * azimuth_cells, azimuth_cells),
                    read(scale, at) * signed_sum(terms),
                )

    make_base(field_a, 0, axial_cells)

    def squeeze(recv, group):
        lanes = lax.broadcasted_iota(I32, (8, LANES), 1)
        parts = []
        for start_block in range(group * half_blocks, (group + 1) * half_blocks, 4):
            b = [recv[start_block + i] for i in range(4)]
            parts.append(jnp.where(lanes < 96, b[0], b[1]))
            parts.append(jnp.where(lanes < 64, b[1], b[2]))
            parts.append(jnp.where(lanes < 32, b[2], b[3]))
        return jnp.concatenate(parts, axis=1)

    def put_hots(group):
        cells = squeeze(cell_recv, group)
        row, column = cells[0:1], cells[1:2]
        put_row[group] = one_hot(
            lax.broadcasted_iota(I32, (rows, half), 0).astype(F32)
            == jnp.broadcast_to(row, (rows, half))
        )
        upright = jnp.broadcast_to(column, (LANES, half)).T
        put_radial[group] = one_hot(
            jnp.concatenate([upright] * tiles, axis=1)
            == lax.broadcasted_iota(I32, (half, radial_cells), 1).astype(F32)
        )
        return row, column

    def add_flames(parts, hot, group):
        left = jnp.concatenate(
            [hot * part[c : c + 1, :] for part in parts for c in range(channels)], axis=0
        )
        totals = jnp.dot(left, put_radial[group], preferred_element_type=F32)
        middle = totals.shape[0] // 2
        return totals[:middle] + totals[middle:]

    chunk = rows // 4

    def subtract_near(step):
        parts = halves(squeeze(flame_recv.at[step], near))
        for top in range(0, rows, chunk):
            at = pl.ds(top, chunk)
            totals = add_flames(parts, put_row[near, top : top + chunk, :], near)
            for c in range(channels):
                write(base, c, at, read(base, c, at) - totals[c * chunk : (c + 1) * chunk])

    wait_blocks(cell_recv, cell_sems, near)
    put_hots(near)
    wait_blocks(flame_recv.at[0], flame_sems.at[0], near)
    subtract_near(0)

    wait_bytes(sound_end, sound_sems.at[1, 1])
    wait_bytes(sound_side, sound_sems.at[1, 0])
    k_axial[first, :] = 0.5 * (
        read(sound, first_rows) + jnp.where(first_axial, 0.0, read(sound_end, 0, whole))
    )
    k_axial[pl.ds(rows, azimuth_cells), :] = 0.5 * (
        read(sound, last_rows) + jnp.where(last_axial, 0.0, read(sound_end, 1, whole))
    )
    for side in range(2):
        for i in range(tiles):
            edge[side, i] = 0.5 * (sound[i, padded_side_rows[side], :] + sound_side[side, i])

    def scales(a, _):
        at = own_rows(a)
        low = jnp.broadcast_to(read(edge, 0, pl.ds(a, 1)), tile)
        high = jnp.broadcast_to(read(edge, 1, pl.ds(a, 1)), tile)
        weights = k_axial[at, :] + k_axial[own_rows(a + 1), :] + k_rest[2, at, :] + k_rest[3, at, :]
        weights = weights + jnp.where(azimuth == 0, low, k_rest[0, at, :])
        weights = weights + jnp.where(azimuth == azimuth_cells - 1, high, k_rest[1, at, :])
        write(scale, at, RELAX / weights)
        return 0

    lax.fori_loop(0, axial_cells, scales, 0, unroll=True)
    all_rows = pl.ds(0, rows)
    picked_scale = pick([read(scale, all_rows)])

    wait_blocks(cell_recv, cell_sems, far)
    row, column = put_hots(far)
    i = lax.broadcasted_iota(I32, (edge_rows, half), 0)
    edge_row = jnp.where(
        i < axial_cells,
        i * azimuth_cells,
        jnp.where(
            i < 2 * axial_cells,
            (i - axial_cells) * azimuth_cells + azimuth_cells - 1,
            jnp.where(
                i < 2 * axial_cells + azimuth_cells,
                i - 2 * axial_cells,
                i - 2 * axial_cells - 2 * azimuth_cells + rows,
            ),
        ),
    )
    put_edge[...] = one_hot(edge_row.astype(F32) == jnp.broadcast_to(row, (edge_rows, half)))
    upright = jnp.broadcast_to(row * radial_cells + column, (LANES, half)).T
    match[...] = one_hot(
        jnp.concatenate([upright] * (flames // LANES), axis=1)
        == jnp.broadcast_to(cell.astype(F32), (half, flames))
    )

    add_halo(0)
    picked_base = pick_field(base, all_rows)

    wait_blocks(flame_recv.at[0], flame_sems.at[0], far)
    parts = halves(squeeze(flame_recv.at[0], far))
    found = jnp.dot(jnp.concatenate(parts, axis=0), match[...], preferred_element_type=F32)
    found = found[:channels] + found[channels:]
    picked = (1.0 - RELAX) * picked_start[...] + picked_scale * (picked_base - found)
    send_flames(picked, 1)

    totals = add_flames(parts, put_edge[...], far)
    for c in range(channels):
        here = c * edge_rows
        for side in range(2):
            for i in range(tiles):
                added = totals[
                    here + side * axial_cells : here + (side + 1) * axial_cells,
                    i * LANES : (i + 1) * LANES,
                ]
                side_send[1, side, c, i] = (1.0 - RELAX) * side_send[0, side, c, i] + scale[
                    i, side_rows[side], :
                ] * (base[c, i, side_rows[side], :] - added)
        here = here + 2 * axial_cells
        for end, at, padded_at in ((0, first, first_rows), (1, last, last_rows)):
            added = totals[here + end * azimuth_cells : here + (end + 1) * azimuth_cells]
            write(
                end_send,
                end,
                c,
                pl.ds(0, azimuth_cells),
                (1.0 - RELAX) * read(field_a, c, padded_at)
                + read(scale, at) * (read(base, c, at) - added),
            )
    sems = halo_sems.at[1]
    start_ends(end_send.at[0], end_send.at[1], end_recv.at[1], sems)
    start_sides(side_send.at[1], side_recv.at[1], sems)

    loaded("direct")
    chunk_cells = chunk // azimuth_cells

    def send_sensitivity(top):
        at = pl.ds(top, chunk)
        padded_at = pl.ds(top + azimuth_cells, chunk)
        terms = []
        for c in range(channels):
            weight = direct[c, at, :].astype(F32)
            write(direct_tiles, c, at, weight)
            terms.append(
                weight
                * ((1.0 - RELAX) * read(field_b, c, padded_at) + read(scale, at) * read(base, c, at))
            )
        write(sens_own, at, signed_sum(terms))
        start_partner(sens_own.at[:, at], sens_other.at[:, at], 0)

    done = 0
    for top in range(0, rows, chunk):
        totals = add_flames(parts, put_row[far, top : top + chunk, :], far)
        at = pl.ds(top, chunk)
        padded_at = pl.ds(top + azimuth_cells, chunk)
        for c in range(channels):
            write(
                field_b,
                c,
                padded_at,
                (1.0 - RELAX) * read(field_a, c, padded_at)
                + read(scale, at) * (read(base, c, at) - totals[c * chunk : (c + 1) * chunk]),
            )
        ready = (top + chunk) // azimuth_cells
        ready = axial_cells if ready == axial_cells else ready - 1
        make_base(field_b, done, ready)
        done = ready
        if top:
            send_sensitivity(top - chunk)
    send_sensitivity(rows - chunk)

    def direct_at_slots(group):
        hot = put_row[group].astype(F32)
        for g in range(2):
            columns = dot_nt(
                direct[g * modes : (g + 1) * modes].reshape(modes * rows, radial_cells),
                put_radial[group],
            ).reshape(modes, rows, half)
            slot_direct[group, g * modes : (g + 1) * modes] = jnp.sum(columns * hot[None], axis=1)

    def start_slots(group):
        products = squeeze(flame_recv.at[1], group) * slot_direct[group]
        slot_own[group] = jnp.sum(products[:modes], axis=0, keepdims=True) - jnp.sum(
            products[modes:], axis=0, keepdims=True
        )
        start_partner(slot_own.at[group], slot_other.at[group], 1 + group)

    direct_at_slots(near)
    direct_at_slots(far)
    wait_blocks(flame_recv.at[1], flame_sems.at[1], near)
    start_slots(near)
    subtract_near(1)
    add_halo(1)
    start_partner(edge_own, edge_other, 3)

    wait_blocks(flame_recv.at[1], flame_sems.at[1], far)
    start_slots(far)
    parts = halves(squeeze(flame_recv.at[1], far))
    for top in range(0, rows, chunk):
        totals = add_flames(parts, put_row[far, top : top + chunk, :], far)
        at = pl.ds(top, chunk)
        padded_at = pl.ds(top + azimuth_cells, chunk)
        for c in range(channels):
            adjoint[c, at, :] = (1.0 - RELAX) * read(field_b, c, padded_at) + read(scale, at) * (
                read(base, c, at) - totals[c * chunk : (c + 1) * chunk]
            )

    def slot_sums(group):
        wait_bytes(slot_other.at[group], sens_sems.at[1, 1 + group])
        parts = halves(slot_own[group] + slot_other[group])
        hot = put_row[group]
        left = jnp.concatenate([hot * part for part in parts], axis=0)
        totals = jnp.dot(left, put_radial[group], preferred_element_type=F32)
        return totals[:rows] + totals[rows:]

    wait_bytes(sens_other, sens_sems.at[1, 0])
    write(
        sens_sum,
        all_rows,
        read(sens_own, all_rows)
        + read(sens_other, all_rows)
        - read(scale, all_rows) * slot_sums(near),
    )
    wait_bytes(edge_other, sens_sems.at[1, 3])
    edges = [edge_own[i] + edge_other[i] for i in range(tiles)]
    for i in range(tiles):
        for end, at in ((0, first), (1, last)):
            low = 2 * axial_cells + end * azimuth_cells
            sens_sum[i, at, :] = sens_sum[i, at, :] + edges[i][low : low + azimuth_cells]
        for side in range(2):
            at = side_rows[side]
            sens_sum[i, at, :] = (
                sens_sum[i, at, :] + edges[i][side * axial_cells : (side + 1) * axial_cells]
            )
    sensitivity[...] = read(sens_sum, all_rows) - read(scale, all_rows) * slot_sums(far)
    for ref, sem in sent:
        wait_bytes(ref, sem)


def local(
    n_sector,
    n_axial,
    rhs,
    adjoint_start,
    sound_sq,
    direct_mode,
    omega_sq,
    flame_gain,
    delay_phase,
    delay_bin,
    flame_cell,
    injector_sector,
    injector_cell,
):
    parts, modes, axial_cells, azimuth_cells, radial_cells = rhs.shape
    channels = parts * modes
    rows = axial_cells * azimuth_cells
    flames = flame_cell.shape[1]
    half = n_sector // 2 * CAP
    tiles = radial_cells // LANES
    block = (channels, rows, radial_cells)
    padded = (channels, tiles, rows + 2 * azimuth_cells, LANES)
    side = (tiles, axial_cells, LANES)
    plane = (rows, radial_cells)
    dma = pltpu.SemaphoreType.DMA
    vmem = pltpu.VMEM
    scratch = [
        vmem(block, F32),
        vmem(padded, F32),
        vmem(padded, F32),
        vmem(padded[1:], F32),
        vmem(block, BF16),
        pltpu.SMEM((2, modes), F32),
        vmem((1, flames), F32),
        vmem(delay_phase.shape, F32),
        vmem((1, flames), I32),
        vmem((1, flames), I32),
        vmem((1, flames), I32),
        vmem((1, flames), I32),
        vmem((channels, tiles, rows, LANES), F32),
        vmem((tiles, rows, LANES), F32),
        vmem((rows + azimuth_cells, radial_cells), F32),
        vmem((4,) + plane, F32),
        vmem((2,) + side, F32),
        vmem((2 * radial_cells, flames), BF16),
        vmem((rows, flames), F32),
        vmem((channels, flames), F32),
        vmem((LANES, flames), BF16),
        vmem((n_sector, flames), F32),
        vmem((modes, flames), F32),
        vmem((modes, flames), F32),
        vmem((2, rows, half), BF16),
        vmem((2 * (axial_cells + azimuth_cells), half), BF16),
        vmem((2, half, radial_cells), BF16),
        vmem((half, flames), BF16),
        vmem((2,) + side, F32),
        vmem((2,) + side, F32),
        vmem((ITERS, 2, channels) + side, F32),
        vmem((ITERS, 2, channels) + side, F32),
        vmem((2, channels, tiles, azimuth_cells, LANES), F32),
        vmem((ITERS, 2, channels, tiles, azimuth_cells, LANES), F32),
        vmem((2, tiles, azimuth_cells, LANES), F32),
        vmem((n_sector, 8, LANES), F32),
        vmem((n_sector, 8, LANES), F32),
        vmem((ITERS, n_sector, 8, LANES), F32),
        vmem((ITERS, n_sector, 8, LANES), F32),
        vmem((channels, tiles, rows, LANES), F32),
        vmem((2, channels, half), F32),
        vmem((tiles, rows, LANES), F32),
        vmem((tiles, rows, LANES), F32),
        vmem((tiles, rows, LANES), F32),
        vmem((tiles, 2 * (axial_cells + azimuth_cells), LANES), F32),
        vmem((tiles, 2 * (axial_cells + azimuth_cells), LANES), F32),
        vmem((2, 1, half), F32),
        vmem((2, 1, half), F32),
        dma((9 + 2 * tiles,)),
        dma((2, 2)),
        dma((ITERS, 2, 2)),
        dma((3,)),
        dma((ITERS, 3)),
        dma((2, 4)),
    ]
    in_hbm = pl.BlockSpec(memory_space=pltpu.HBM)

    def stay(array):
        return pltpu.with_memory_space_constraint(array, pltpu.HBM)

    in_vmem = pl.BlockSpec(memory_space=pltpu.VMEM)
    adjoint, sensitivity = pl.pallas_call(
        functools.partial(
            kernel, n_sector, n_axial, (modes, axial_cells, azimuth_cells, radial_cells)
        ),
        out_shape=(jax.ShapeDtypeStruct(block, F32), jax.ShapeDtypeStruct(plane, F32)),
        in_specs=[in_hbm] * 11,
        out_specs=(in_vmem, in_vmem),
        scratch_shapes=scratch,
        compiler_params=pltpu.CompilerParams(
            collective_id=0, has_side_effects=True, vmem_limit_bytes=40 * 1024 * 1024
        ),
        name="helmholtz_steps",
    )(
        stay(rhs.reshape(block)),
        stay(adjoint_start.reshape(block)),
        stay(sound_sq.reshape(plane)),
        stay(direct_mode.reshape(block)),
        stay(omega_sq),
        stay(flame_gain),
        stay(delay_phase),
        stay(delay_bin),
        stay(flame_cell),
        stay(injector_sector.reshape(1, flames)),
        stay(injector_cell),
    )
    return adjoint.reshape(rhs.shape), sensitivity.reshape(sound_sq.shape)


def solution(mesh):
    placed = (
        P(None, "modes", "axial", "sector", None),
        P(None, "modes", "axial", "sector", None),
        P("axial", "sector", None),
        P(None, "modes", "axial", "sector", None),
        P(None, "modes"),
        P("axial", "sector"),
        P("modes", None),
        P("axial", "sector"),
        P("axial", "sector"),
        P("axial", "sector", None),
        P("axial", "sector"),
    )
    return jax.shard_map(
        functools.partial(local, mesh.shape["sector"], mesh.shape["axial"]),
        mesh=mesh,
        in_specs=placed,
        out_specs=(P(None, "modes", "axial", "sector", None), P("axial", "sector", None)),
        check_vma=False,
    )
```

```python
import functools

import jax
import jax.numpy as jnp
from jax import lax
from jax.experimental import pallas as pl
from jax.experimental.pallas import tpu as pltpu
from jax.sharding import PartitionSpec as P

ITERS = 2
RELAX = 0.6
CAP = 96
LANES = 128
MESH = pl.DeviceIdType.MESH
BF16 = jnp.bfloat16
F32 = jnp.float32
I32 = jnp.int32


def one_hot(flags):
    return jnp.where(flags, 1.0, 0.0).astype(BF16)


def halves(values):
    high = values.astype(BF16)
    return high, (values - high.astype(F32)).astype(BF16)


def dot_nt(left, right):
    return lax.dot_general(
        left, right, (((1,), (1,)), ((), ())), preferred_element_type=F32
    )


def read(ref, *index):
    *lead, at = index
    tiles = ref.shape[len(lead)]
    return jnp.concatenate([ref[(*lead, i, at)] for i in range(tiles)], axis=-1)


def write(ref, *index_and_value):
    *lead, at, value = index_and_value
    for i in range(ref.shape[len(lead)]):
        ref[(*lead, i, at)] = value[..., i * LANES : (i + 1) * LANES]


def flip(sector, mask, n_sector):
    bit = 1
    other = sector
    while bit < n_sector:
        if mask & bit:
            other = other + bit * (1 - 2 * (sector // bit % 2))
        bit *= 2
    return other


def partner_order(n_sector):
    hops = {mask: (0, 1, 2, 1)[mask // 2 % 4] + mask // 8 for mask in range(n_sector)}
    return sorted(range(n_sector), key=lambda mask: (hops[mask], mask))


def kernel(
    n_sector,
    n_axial,
    shape,
    rhs_hbm,
    start_hbm,
    sound_hbm,
    direct_hbm,
    omega_hbm,
    gain_hbm,
    phase_hbm,
    bin_hbm,
    source_hbm,
    sector_hbm,
    target_hbm,
    adjoint,
    sensitivity,
    rhs,
    field_a,
    field_b,
    sound,
    direct,
    omega,
    gain,
    phase,
    bins,
    source,
    sector,
    target,
    base,
    scale,
    k_axial,
    k_rest,
    edge,
    pick_radial,
    pick_row,
    picked_start,
    picked_base,
    edge_pick,
    lane_hot,
    block_hot,
    gain_cos,
    gain_sin,
    put_row,
    put_edge,
    put_radial,
    match,
    sound_send,
    sound_side,
    side_send,
    side_recv,
    end_send,
    end_recv,
    sound_end,
    cell_send,
    cell_recv,
    flame_send,
    flame_recv,
    direct_tiles,
    slot_direct,
    sens_own,
    sens_other,
    sens_sum,
    edge_own,
    edge_other,
    slot_own,
    slot_other,
    in_sem,
    sound_sems,
    halo_sems,
    cell_sems,
    flame_sems,
    sens_sems,
):
    modes, axial_cells, azimuth_cells, radial_cells = shape
    channels = 2 * modes
    rows = axial_cells * azimuth_cells
    flames = gain.shape[1]
    tiles = radial_cells // LANES
    half_blocks = n_sector // 2
    half = half_blocks * CAP
    near, far = 0, 1
    axial = lax.axis_index("axial")
    my_sector = lax.axis_index("sector")
    my_modes = lax.axis_index("modes")
    up_axial = lax.rem(axial + 1, n_axial)
    down_axial = lax.rem(axial + n_axial - 1, n_axial)
    next_sector = lax.rem(my_sector + 1, n_sector)
    last_sector = lax.rem(my_sector + n_sector - 1, n_sector)
    partners = [flip(my_sector, mask, n_sector) for mask in partner_order(n_sector)]

    barrier = pltpu.get_barrier_semaphore()
    for other in partners[1:]:
        pl.semaphore_signal(barrier, inc=1, device_id={"sector": other}, device_id_type=MESH)
    for other in (next_sector, last_sector):
        pl.semaphore_signal(barrier, inc=1, device_id={"sector": other}, device_id_type=MESH)
    for other in (up_axial, down_axial):
        pl.semaphore_signal(barrier, inc=1, device_id={"axial": other}, device_id_type=MESH)
    pl.semaphore_signal(
        barrier, inc=1, device_id={"modes": 1 - my_modes}, device_id_type=MESH
    )

    inner = pl.ds(azimuth_cells, rows)
    pieces = [pl.ds(i * LANES, LANES) for i in range(tiles)]
    loads = {}
    for name, source_ref, target_ref in (
        [("sector", sector_hbm, sector), ("target", target_hbm, target), ("source", source_hbm, source)]
        + [("bins", bin_hbm, bins), ("phase", phase_hbm, phase), ("gain", gain_hbm, gain)]
        + [(("sound", i), sound_hbm.at[:, pieces[i]], sound.at[i, inner]) for i in range(tiles)]
        + [(("start", i), start_hbm.at[:, :, pieces[i]], field_a.at[:, i, inner]) for i in range(tiles)]
        + [("omega", omega_hbm, omega), ("rhs", rhs_hbm, rhs), ("direct", direct_hbm, direct)]
    ):
        loads[name] = pltpu.make_async_copy(source_ref, target_ref, in_sem.at[len(loads)])
        if name not in ("rhs", "direct"):
            loads[name].start()

    def loaded(*names):
        for name in names:
            loads[name].wait()

    loaded("sector", "target", "source")
    partner = jnp.zeros((n_sector, LANES), I32)
    position = lax.broadcasted_iota(I32, (n_sector, LANES), 0)
    for p, other in enumerate(partners):
        partner = jnp.where(position == p, other, partner)
    partner = jnp.concatenate([partner] * (flames // LANES), axis=1)
    in_block = jnp.where(jnp.broadcast_to(sector[...], (n_sector, flames)) == partner, 1.0, 0.0)
    block_hot[...] = in_block
    before = one_hot(
        lax.broadcasted_iota(I32, (flames, flames), 0)
        < lax.broadcasted_iota(I32, (flames, flames), 1)
    )
    earlier = jnp.dot(in_block.astype(BF16), before, preferred_element_type=F32)
    rank = jnp.sum(in_block * earlier, axis=0, keepdims=True).astype(I32)
    block_of = jnp.sum(
        in_block * lax.broadcasted_iota(I32, (n_sector, flames), 0).astype(F32),
        axis=0,
        keepdims=True,
    ).astype(I32)
    lane = (rank + CAP * block_of) & (LANES - 1)
    lane_hot[...] = one_hot(
        lax.broadcasted_iota(I32, (LANES, flames), 0) == jnp.broadcast_to(lane, (LANES, flames))
    )

    def pack(parts):
        left = jnp.concatenate(
            [
                jnp.concatenate(
                    [part * block_hot[p : p + 1, :] for p in range(n_sector)], axis=0
                ).astype(BF16)
                for part in parts
            ],
            axis=0,
        )
        packed = dot_nt(left, lane_hot[...])
        total = packed[: 8 * n_sector]
        for i in range(1, len(parts)):
            total = total + packed[8 * n_sector * i : 8 * n_sector * (i + 1)]
        return total.reshape(n_sector, 8, LANES)

    target_row = (target[...] // radial_cells).astype(F32)
    target_radial = (target[...] % radial_cells).astype(F32)
    sub = lax.broadcasted_iota(I32, (8, flames), 0)
    cell_send[...] = pack(
        [
            jnp.where(
                sub == 0,
                jnp.broadcast_to(target_row, (8, flames)),
                jnp.where(sub == 1, jnp.broadcast_to(target_radial, (8, flames)), 0.0),
            )
        ]
    )

    def remote(src, dst, send_sem, recv_sem, device):
        return pltpu.make_async_remote_copy(
            src_ref=src,
            dst_ref=dst,
            send_sem=send_sem,
            recv_sem=recv_sem,
            device_id=device,
            device_id_type=MESH,
        )

    def wait_bytes(ref, sem):
        pltpu.make_async_copy(ref, ref, sem).wait()

    first_rows = pl.ds(azimuth_cells, azimuth_cells)
    last_rows = pl.ds(rows, azimuth_cells)
    sent = []

    def start_sides(send, recv, sems):
        remote(send.at[1], recv.at[0], sems.at[0, 0], sems.at[1, 0], {"sector": next_sector}).start()
        remote(send.at[0], recv.at[1], sems.at[0, 0], sems.at[1, 0], {"sector": last_sector}).start()
        sent.append((recv, sems.at[0, 0]))

    def start_ends(first, last, recv, sems):
        remote(last, recv.at[0], sems.at[0, 1], sems.at[1, 1], {"axial": up_axial}).start()
        remote(first, recv.at[1], sems.at[0, 1], sems.at[1, 1], {"axial": down_axial}).start()
        sent.append((recv, sems.at[0, 1]))

    def start_blocks(send, recv, sems):
        for p in reversed(range(1, n_sector)):
            group = 0 if p < half_blocks else 1
            remote(
                send.at[p], recv.at[p], sems.at[2], sems.at[group], {"sector": partners[p]}
            ).start()
        sent.append((send.at[pl.ds(1, n_sector - 1)], sems.at[2]))

    def wait_blocks(recv, sems, group):
        start = max(1, group * half_blocks)
        wait_bytes(recv.at[pl.ds(start, (group + 1) * half_blocks - start)], sems.at[group])

    def start_partner(send, recv, i):
        remote(
            send, recv, sens_sems.at[0, i], sens_sems.at[1, i], {"modes": 1 - my_modes}
        ).start()
        sent.append((send, sens_sems.at[0, i]))

    side_rows = [
        pl.ds(row, axial_cells, azimuth_cells) for row in (0, azimuth_cells - 1)
    ]
    padded_side_rows = [
        pl.ds(azimuth_cells + row, axial_cells, azimuth_cells) for row in (0, azimuth_cells - 1)
    ]

    cell = source[...]
    row_of = jnp.broadcast_to(cell // radial_cells, (rows, flames))
    pick_row[...] = jnp.where(lax.broadcasted_iota(I32, (rows, flames), 0) == row_of, 1.0, 0.0)
    radial_of = jnp.broadcast_to(cell % radial_cells, (radial_cells, flames))
    radial_hot = one_hot(lax.broadcasted_iota(I32, (radial_cells, flames), 0) == radial_of)
    pick_radial[:radial_cells] = radial_hot
    pick_radial[radial_cells:] = radial_hot

    loaded("bins", "phase", "gain")
    bin_count = phase.shape[1]
    bin_hot = jnp.where(
        lax.broadcasted_iota(I32, (bin_count, flames), 0)
        == jnp.broadcast_to(bins[...], (bin_count, flames)),
        1.0,
        0.0,
    )
    angle = phase[...]
    gains = jnp.broadcast_to(gain[...], (modes, flames))
    exact = lax.Precision.HIGHEST
    gain_cos[...] = gains * jnp.dot(
        jnp.cos(angle), bin_hot, precision=exact, preferred_element_type=F32
    )
    gain_sin[...] = -gains * jnp.dot(
        jnp.sin(angle), bin_hot, precision=exact, preferred_element_type=F32
    )

    loaded(*[("sound", i) for i in range(tiles)])
    for side in range(2):
        for i in range(tiles):
            sound_send[side, i] = sound[i, padded_side_rows[side], :]

    pl.semaphore_wait(barrier, n_sector + 4)

    start_blocks(cell_send, cell_recv, cell_sems)
    start_ends(sound.at[:, first_rows], sound.at[:, last_rows], sound_end, sound_sems)
    start_sides(sound_send, sound_side, sound_sems)
    cell_recv[0] = cell_send[0]

    loaded(*[("start", i) for i in range(tiles)])
    loads["rhs"].start()
    sems = halo_sems.at[0]
    start_ends(field_a.at[:, :, first_rows], field_a.at[:, :, last_rows], end_recv.at[0], sems)
    for side in range(2):
        for c in range(channels):
            for i in range(tiles):
                side_send[0, side, c, i] = field_a[c, i, padded_side_rows[side], :]
    start_sides(side_send.at[0], side_recv.at[0], sems)

    def pick(planes, hot=pick_row):
        high, low = halves(jnp.concatenate(planes, axis=0))
        columns = jnp.dot(
            jnp.concatenate([high, low], axis=1), pick_radial[...], preferred_element_type=F32
        ).reshape(len(planes), hot.shape[0], flames)
        return jnp.sum(columns * hot[...][None], axis=1)

    def pick_field(ref, at):
        return jnp.concatenate(
            [
                pick([read(ref, g * modes + m, at) for m in range(modes)])
                for g in range(2)
            ],
            axis=0,
        )

    def send_flames(picked, step):
        real, imag = picked[:modes], picked[modes:]
        cosines, sines = gain_cos[...], gain_sin[...]
        amounts = jnp.concatenate(
            [cosines * real - sines * imag, cosines * imag + sines * real], axis=0
        )
        high = amounts.astype(BF16).astype(F32)
        flame_send[step] = pack([high, amounts - high])
        start_blocks(flame_send.at[step], flame_recv.at[step], flame_sems.at[step])
        flame_recv[step, 0] = flame_send[step, 0]

    picked_start[...] = pick_field(field_a, inner)
    send_flames(picked_start[...], 0)

    tile = (azimuth_cells, radial_cells)
    azimuth = lax.broadcasted_iota(I32, tile, 0)
    radial = lax.broadcasted_iota(I32, tile, 1)

    def own_rows(a):
        if isinstance(a, int):
            return pl.ds(a * azimuth_cells, azimuth_cells)
        return pl.ds(pl.multiple_of(a * azimuth_cells, azimuth_cells), azimuth_cells)

    def couplings(a, _):
        s = read(sound, own_rows(a + 1))
        at = own_rows(a)
        k_rest[0, at, :] = jnp.where(azimuth == 0, 0.0, 0.5 * (s + pltpu.roll(s, 1, 0)))
        k_rest[1, at, :] = jnp.where(
            azimuth == azimuth_cells - 1, 0.0, 0.5 * (s + pltpu.roll(s, azimuth_cells - 1, 0))
        )
        k_rest[2, at, :] = jnp.where(radial == 0, 0.0, 0.5 * (s + pltpu.roll(s, 1, 1)))
        k_rest[3, at, :] = jnp.where(
            radial == radial_cells - 1, 0.0, 0.5 * (s + pltpu.roll(s, radial_cells - 1, 1))
        )
        return 0

    def axial_coupling(a, _):
        k_axial[own_rows(a), :] = 0.5 * (read(sound, own_rows(a)) + read(sound, own_rows(a + 1)))
        return 0

    lax.fori_loop(0, axial_cells, couplings, 0, unroll=True)
    lax.fori_loop(1, axial_cells, axial_coupling, 0, unroll=True)

    loaded("omega", "rhs")
    loads["direct"].start()
    omega_real = [omega[0, m] for m in range(modes)]
    omega_imag = [omega[1, m] for m in range(modes)]

    def base_rows(field, a, modes_here):
        low, high = a > 0, a < axial_cells - 1
        at, mid, top = own_rows(a), own_rows(a + 1), own_rows(a + 2)
        k_slo, k_shi, k_rlo, k_rhi = (k_rest[i, at, :] for i in range(4))
        k_alo = k_axial[at, :] if low else None
        k_ahi = k_axial[mid, :] if high else None
        for m in modes_here:
            real, imag = read(field, m, mid), read(field, modes + m, mid)
            for c, x, mass in (
                (m, real, omega_real[m] * real - omega_imag[m] * imag),
                (modes + m, imag, omega_real[m] * imag + omega_imag[m] * real),
            ):
                total = rhs[c, at, :] + mass
                if low:
                    total = total + k_alo * read(field, c, at)
                if high:
                    total = total + k_ahi * read(field, c, top)
                total = total + k_slo * pltpu.roll(x, 1, 0)
                total = total + k_shi * pltpu.roll(x, azimuth_cells - 1, 0)
                total = total + k_rlo * pltpu.roll(x, 1, 1)
                total = total + k_rhi * pltpu.roll(x, radial_cells - 1, 1)
                write(base, c, at, total)

    def make_base(field, low, high):
        for a in range(low, high):
            base_rows(field, a, range(modes))

    first_axial = axial == 0
    last_axial = axial == n_axial - 1
    first, last = pl.ds(0, azimuth_cells), pl.ds(rows - azimuth_cells, azimuth_cells)
    whole = pl.ds(0, azimuth_cells)

    edge_rows = 2 * axial_cells + 2 * azimuth_cells

    def signed_sum(terms):
        return sum(terms[1:modes], terms[0]) - sum(terms[modes + 1 :], terms[modes])

    def add_halo(step):
        wait_bytes(end_recv.at[step], halo_sems.at[step, 1, 1])
        k_low = k_axial[pl.ds(0, azimuth_cells), :]
        k_high = k_axial[pl.ds(rows, azimuth_cells), :]
        low_terms, high_terms, planes = [], [], [[] for _ in range(channels)]
        for c in range(channels):
            below = k_low * jnp.where(first_axial, 0.0, read(end_recv, step, 0, c, whole))
            above = k_high * jnp.where(last_axial, 0.0, read(end_recv, step, 1, c, whole))
            write(base, c, first, read(base, c, first) + below)
            write(base, c, last, read(base, c, last) + above)
            planes[c] += [below, above]
            if step == ITERS - 1:
                low_terms.append(below * read(direct_tiles, c, first))
                high_terms.append(above * read(direct_tiles, c, last))
        wait_bytes(side_recv.at[step], halo_sems.at[step, 1, 0])
        for side in range(2):
            at = side_rows[side]
            sides = [[] for _ in range(channels)]
            for i in range(tiles):
                terms = []
                for c in range(channels):
                    added = edge[side, i] * side_recv[step, side, c, i]
                    sides[c].append(added)
                    base[c, i, at, :] = base[c, i, at, :] + added
                    if step == ITERS - 1:
                        terms.append(added * direct_tiles[c, i, at, :])
                if step == ITERS - 1:
                    edge_own[i, pl.ds(side * axial_cells, axial_cells), :] = scale[
                        i, at, :
                    ] * signed_sum(terms)
            for c in range(channels):
                planes[c].insert(side, jnp.concatenate(sides[c], axis=1))
        if step < ITERS - 1:
            return [jnp.concatenate(parts, axis=0) for parts in planes]
        if step == ITERS - 1:
            for end, at, terms in ((0, first, low_terms), (1, last, high_terms)):
                write(
                    edge_own,
                    pl.ds(2 * axial_cells + end * azimuth_cells, azimuth_cells),
                    read(scale, at) * signed_sum(terms),
                )

    all_rows = pl.ds(0, rows)
    real_base, imag_base = [], []
    for m in range(modes):
        for a in range(axial_cells):
            base_rows(field_a, a, [m])
        pair = pick([read(base, m, all_rows), read(base, modes + m, all_rows)])
        real_base.append(pair[0:1])
        imag_base.append(pair[1:2])
    picked_base[...] = jnp.concatenate(real_base + imag_base, axis=0)

    def squeeze(recv, group):
        lanes = lax.broadcasted_iota(I32, (8, LANES), 1)
        parts = []
        for start_block in range(group * half_blocks, (group + 1) * half_blocks, 4):
            b = [recv[start_block + i] for i in range(4)]
            parts.append(jnp.where(lanes < 96, b[0], b[1]))
            parts.append(jnp.where(lanes < 64, b[1], b[2]))
            parts.append(jnp.where(lanes < 32, b[2], b[3]))
        return jnp.concatenate(parts, axis=1)

    def put_hots(group):
        cells = squeeze(cell_recv, group)
        row, column = cells[0:1], cells[1:2]
        put_row[group] = one_hot(
            lax.broadcasted_iota(I32, (rows, half), 0).astype(F32)
            == jnp.broadcast_to(row, (rows, half))
        )
        upright = jnp.broadcast_to(column, (LANES, half)).T
        put_radial[group] = one_hot(
            jnp.concatenate([upright] * tiles, axis=1)
            == lax.broadcasted_iota(I32, (half, radial_cells), 1).astype(F32)
        )
        return row, column

    def add_flames(parts, hot, group):
        left = jnp.concatenate(
            [hot * part[c : c + 1, :] for part in parts for c in range(channels)], axis=0
        )
        totals = jnp.dot(left, put_radial[group], preferred_element_type=F32)
        middle = totals.shape[0] // 2
        return totals[:middle] + totals[middle:]

    chunk = rows // 4

    i = lax.broadcasted_iota(I32, (edge_rows, LANES), 0)
    edge_row = jnp.where(
        i < axial_cells,
        i * azimuth_cells,
        jnp.where(
            i < 2 * axial_cells,
            (i - axial_cells) * azimuth_cells + azimuth_cells - 1,
            jnp.where(
                i < 2 * axial_cells + azimuth_cells,
                i - 2 * axial_cells,
                i - 2 * axial_cells - 2 * azimuth_cells + rows,
            ),
        ),
    ).astype(F32)
    flame_row = (cell // radial_cells).astype(F32)
    edge_pick[...] = jnp.where(
        jnp.concatenate([edge_row] * (flames // LANES), axis=1)
        == jnp.broadcast_to(flame_row, (edge_rows, flames)),
        1.0,
        0.0,
    )

    def all_hots(group):
        row, column = put_hots(group)
        put_edge[group] = one_hot(
            jnp.concatenate([edge_row] * (half // LANES), axis=1)
            == jnp.broadcast_to(row, (edge_rows, half))
        )
        upright = jnp.broadcast_to(row * radial_cells + column, (LANES, half)).T
        match[group] = one_hot(
            jnp.concatenate([upright] * (flames // LANES), axis=1)
            == jnp.broadcast_to(cell.astype(F32), (half, flames))
        )

    def found_at_flames(parts, group):
        found = jnp.dot(jnp.concatenate(parts, axis=0), match[group], preferred_element_type=F32)
        return found[:channels] + found[channels:]

    wait_blocks(cell_recv, cell_sems, near)
    all_hots(near)

    wait_bytes(sound_end, sound_sems.at[1, 1])
    wait_bytes(sound_side, sound_sems.at[1, 0])
    k_axial[first, :] = 0.5 * (
        read(sound, first_rows) + jnp.where(first_axial, 0.0, read(sound_end, 0, whole))
    )
    k_axial[pl.ds(rows, azimuth_cells), :] = 0.5 * (
        read(sound, last_rows) + jnp.where(last_axial, 0.0, read(sound_end, 1, whole))
    )
    for side in range(2):
        for i in range(tiles):
            edge[side, i] = 0.5 * (sound[i, padded_side_rows[side], :] + sound_side[side, i])

    def scales(a, _):
        at = own_rows(a)
        low = jnp.broadcast_to(read(edge, 0, pl.ds(a, 1)), tile)
        high = jnp.broadcast_to(read(edge, 1, pl.ds(a, 1)), tile)
        weights = k_axial[at, :] + k_axial[own_rows(a + 1), :] + k_rest[2, at, :] + k_rest[3, at, :]
        weights = weights + jnp.where(azimuth == 0, low, k_rest[0, at, :])
        weights = weights + jnp.where(azimuth == azimuth_cells - 1, high, k_rest[1, at, :])
        write(scale, at, RELAX / weights)
        return 0

    lax.fori_loop(0, axial_cells, scales, 0, unroll=True)
    picked_scale = pick([read(scale, all_rows)])

    wait_blocks(cell_recv, cell_sems, far)
    all_hots(far)
    wait_blocks(flame_recv.at[0], flame_sems.at[0], near)
    near_parts = halves(squeeze(flame_recv.at[0], near))
    found_near = found_at_flames(near_parts, near)
    planes = add_halo(0)
    inside = picked_base[...] - found_near + pick(planes, edge_pick)

    edge_totals = add_flames(near_parts, put_edge[near], near)

    wait_blocks(flame_recv.at[0], flame_sems.at[0], far)
    parts = halves(squeeze(flame_recv.at[0], far))
    picked = (1.0 - RELAX) * picked_start[...] + picked_scale * (
        inside - found_at_flames(parts, far)
    )
    send_flames(picked, 1)

    totals = edge_totals + add_flames(parts, put_edge[far], far)
    for c in range(channels):
        here = c * edge_rows
        for side in range(2):
            for i in range(tiles):
                added = totals[
                    here + side * axial_cells : here + (side + 1) * axial_cells,
                    i * LANES : (i + 1) * LANES,
                ]
                side_send[1, side, c, i] = (1.0 - RELAX) * side_send[0, side, c, i] + scale[
                    i, side_rows[side], :
                ] * (base[c, i, side_rows[side], :] - added)
        here = here + 2 * axial_cells
        for end, at, padded_at in ((0, first, first_rows), (1, last, last_rows)):
            added = totals[here + end * azimuth_cells : here + (end + 1) * azimuth_cells]
            write(
                end_send,
                end,
                c,
                pl.ds(0, azimuth_cells),
                (1.0 - RELAX) * read(field_a, c, padded_at)
                + read(scale, at) * (read(base, c, at) - added),
            )
    sems = halo_sems.at[1]
    start_ends(end_send.at[0], end_send.at[1], end_recv.at[1], sems)
    start_sides(side_send.at[1], side_recv.at[1], sems)

    loaded("direct")
    chunk_cells = chunk // azimuth_cells

    def send_sensitivity(top):
        at = pl.ds(top, chunk)
        padded_at = pl.ds(top + azimuth_cells, chunk)
        terms = []
        for c in range(channels):
            weight = direct[c, at, :].astype(F32)
            write(direct_tiles, c, at, weight)
            terms.append(
                weight
                * ((1.0 - RELAX) * read(field_b, c, padded_at) + read(scale, at) * read(base, c, at))
            )
        write(sens_own, at, signed_sum(terms))
        start_partner(sens_own.at[:, at], sens_other.at[:, at], 0)

    done = 0
    for top in range(0, rows, chunk):
        totals = add_flames(near_parts, put_row[near, top : top + chunk, :], near)
        totals = totals + add_flames(parts, put_row[far, top : top + chunk, :], far)
        at = pl.ds(top, chunk)
        padded_at = pl.ds(top + azimuth_cells, chunk)
        for c in range(channels):
            write(
                field_b,
                c,
                padded_at,
                (1.0 - RELAX) * read(field_a, c, padded_at)
                + read(scale, at) * (read(base, c, at) - totals[c * chunk : (c + 1) * chunk]),
            )
        ready = (top + chunk) // azimuth_cells
        ready = axial_cells if ready == axial_cells else ready - 1
        make_base(field_b, done, ready)
        done = ready
        if top:
            send_sensitivity(top - chunk)
    send_sensitivity(rows - chunk)

    def direct_at_slots(group):
        hot = put_row[group].astype(F32)
        for g in range(2):
            columns = dot_nt(
                direct[g * modes : (g + 1) * modes].reshape(modes * rows, radial_cells),
                put_radial[group],
            ).reshape(modes, rows, half)
            slot_direct[group, g * modes : (g + 1) * modes] = jnp.sum(columns * hot[None], axis=1)

    direct_at_slots(near)
    direct_at_slots(far)
    add_halo(1)
    start_partner(edge_own, edge_other, 2)
    parts = []
    for group in (near, far):
        wait_blocks(flame_recv.at[1], flame_sems.at[1], group)
        amounts = squeeze(flame_recv.at[1], group)
        products = amounts * slot_direct[group]
        slot_own[group] = jnp.sum(products[:modes], axis=0, keepdims=True) - jnp.sum(
            products[modes:], axis=0, keepdims=True
        )
        parts.append(halves(amounts))
    start_partner(slot_own, slot_other, 1)
    for top in range(0, rows, chunk):
        totals = add_flames(parts[near], put_row[near, top : top + chunk, :], near)
        totals = totals + add_flames(parts[far], put_row[far, top : top + chunk, :], far)
        at = pl.ds(top, chunk)
        padded_at = pl.ds(top + azimuth_cells, chunk)
        for c in range(channels):
            adjoint[c, at, :] = (1.0 - RELAX) * read(field_b, c, padded_at) + read(scale, at) * (
                read(base, c, at) - totals[c * chunk : (c + 1) * chunk]
            )

    wait_bytes(sens_other, sens_sems.at[1, 0])
    write(sens_sum, all_rows, read(sens_own, all_rows) + read(sens_other, all_rows))
    wait_bytes(edge_other, sens_sems.at[1, 2])
    edges = [edge_own[i] + edge_other[i] for i in range(tiles)]
    for i in range(tiles):
        for end, at in ((0, first), (1, last)):
            low = 2 * axial_cells + end * azimuth_cells
            sens_sum[i, at, :] = sens_sum[i, at, :] + edges[i][low : low + azimuth_cells]
        for side in range(2):
            at = side_rows[side]
            sens_sum[i, at, :] = (
                sens_sum[i, at, :] + edges[i][side * axial_cells : (side + 1) * axial_cells]
            )
    wait_bytes(slot_other, sens_sems.at[1, 1])
    slot_totals = 0.0
    for group in (near, far):
        left = jnp.concatenate(
            [put_row[group] * part for part in halves(slot_own[group] + slot_other[group])], axis=0
        )
        totals = jnp.dot(left, put_radial[group], preferred_element_type=F32)
        slot_totals = slot_totals + totals[:rows] + totals[rows:]
    sensitivity[...] = read(sens_sum, all_rows) - read(scale, all_rows) * slot_totals
    for ref, sem in sent:
        wait_bytes(ref, sem)


def hand_over(adjoint_in, sensitivity_in, adjoint_out, sensitivity_out, sems):
    copies = [
        pltpu.make_async_copy(sensitivity_in, sensitivity_out, sems.at[0]),
        pltpu.make_async_copy(adjoint_in, adjoint_out, sems.at[1]),
    ]
    for copy in copies:
        copy.start()
    for copy in copies:
        copy.wait()


def local(
    n_sector,
    n_axial,
    rhs,
    adjoint_start,
    sound_sq,
    direct_mode,
    omega_sq,
    flame_gain,
    delay_phase,
    delay_bin,
    flame_cell,
    injector_sector,
    injector_cell,
):
    parts, modes, axial_cells, azimuth_cells, radial_cells = rhs.shape
    channels = parts * modes
    rows = axial_cells * azimuth_cells
    flames = flame_cell.shape[1]
    half = n_sector // 2 * CAP
    tiles = radial_cells // LANES
    block = (channels, rows, radial_cells)
    padded = (channels, tiles, rows + 2 * azimuth_cells, LANES)
    side = (tiles, axial_cells, LANES)
    plane = (rows, radial_cells)
    dma = pltpu.SemaphoreType.DMA
    vmem = pltpu.VMEM
    scratch = [
        vmem(block, F32),
        vmem(padded, F32),
        vmem(padded, F32),
        vmem(padded[1:], F32),
        vmem(block, BF16),
        pltpu.SMEM((2, modes), F32),
        vmem((1, flames), F32),
        vmem(delay_phase.shape, F32),
        vmem((1, flames), I32),
        vmem((1, flames), I32),
        vmem((1, flames), I32),
        vmem((1, flames), I32),
        vmem((channels, tiles, rows, LANES), F32),
        vmem((tiles, rows, LANES), F32),
        vmem((rows + azimuth_cells, radial_cells), F32),
        vmem((4,) + plane, F32),
        vmem((2,) + side, F32),
        vmem((2 * radial_cells, flames), BF16),
        vmem((rows, flames), F32),
        vmem((channels, flames), F32),
        vmem((channels, flames), F32),
        vmem((2 * (axial_cells + azimuth_cells), flames), F32),
        vmem((LANES, flames), BF16),
        vmem((n_sector, flames), F32),
        vmem((modes, flames), F32),
        vmem((modes, flames), F32),
        vmem((2, rows, half), BF16),
        vmem((2, 2 * (axial_cells + azimuth_cells), half), BF16),
        vmem((2, half, radial_cells), BF16),
        vmem((2, half, flames), BF16),
        vmem((2,) + side, F32),
        vmem((2,) + side, F32),
        vmem((ITERS, 2, channels) + side, F32),
        vmem((ITERS, 2, channels) + side, F32),
        vmem((2, channels, tiles, azimuth_cells, LANES), F32),
        vmem((ITERS, 2, channels, tiles, azimuth_cells, LANES), F32),
        vmem((2, tiles, azimuth_cells, LANES), F32),
        vmem((n_sector, 8, LANES), F32),
        vmem((n_sector, 8, LANES), F32),
        vmem((ITERS, n_sector, 8, LANES), F32),
        vmem((ITERS, n_sector, 8, LANES), F32),
        vmem((channels, tiles, rows, LANES), F32),
        vmem((2, channels, half), F32),
        vmem((tiles, rows, LANES), F32),
        vmem((tiles, rows, LANES), F32),
        vmem((tiles, rows, LANES), F32),
        vmem((tiles, 2 * (axial_cells + azimuth_cells), LANES), F32),
        vmem((tiles, 2 * (axial_cells + azimuth_cells), LANES), F32),
        vmem((2, 1, half), F32),
        vmem((2, 1, half), F32),
        dma((9 + 2 * tiles,)),
        dma((2, 2)),
        dma((ITERS, 2, 2)),
        dma((3,)),
        dma((ITERS, 3)),
        dma((2, 3)),
    ]
    in_hbm = pl.BlockSpec(memory_space=pltpu.HBM)

    def stay(array):
        return pltpu.with_memory_space_constraint(array, pltpu.HBM)

    in_vmem = pl.BlockSpec(memory_space=pltpu.VMEM)
    adjoint, sensitivity = pl.pallas_call(
        functools.partial(
            kernel, n_sector, n_axial, (modes, axial_cells, azimuth_cells, radial_cells)
        ),
        out_shape=(jax.ShapeDtypeStruct(block, F32), jax.ShapeDtypeStruct(plane, F32)),
        in_specs=[in_hbm] * 11,
        out_specs=(in_vmem, in_vmem),
        scratch_shapes=scratch,
        compiler_params=pltpu.CompilerParams(
            collective_id=0, has_side_effects=True, vmem_limit_bytes=40 * 1024 * 1024
        ),
        name="helmholtz_steps",
    )(
        stay(rhs.reshape(block)),
        stay(adjoint_start.reshape(block)),
        stay(sound_sq.reshape(plane)),
        stay(direct_mode.reshape(block)),
        stay(omega_sq),
        stay(flame_gain),
        stay(delay_phase),
        stay(delay_bin),
        stay(flame_cell),
        stay(injector_sector.reshape(1, flames)),
        stay(injector_cell),
    )
    adjoint, sensitivity = pl.pallas_call(
        hand_over,
        out_shape=(jax.ShapeDtypeStruct(block, F32), jax.ShapeDtypeStruct(plane, F32)),
        in_specs=[in_vmem] * 2,
        out_specs=(in_hbm, in_hbm),
        scratch_shapes=[dma((2,))],
        name="hand_over",
    )(
        pltpu.with_memory_space_constraint(adjoint, pltpu.VMEM),
        pltpu.with_memory_space_constraint(sensitivity, pltpu.VMEM),
    )
    return adjoint.reshape(rhs.shape), sensitivity.reshape(sound_sq.shape)


def solution(mesh):
    placed = (
        P(None, "modes", "axial", "sector", None),
        P(None, "modes", "axial", "sector", None),
        P("axial", "sector", None),
        P(None, "modes", "axial", "sector", None),
        P(None, "modes"),
        P("axial", "sector"),
        P("modes", None),
        P("axial", "sector"),
        P("axial", "sector"),
        P("axial", "sector", None),
        P("axial", "sector"),
    )
    return jax.shard_map(
        functools.partial(local, mesh.shape["sector"], mesh.shape["axial"]),
        mesh=mesh,
        in_specs=placed,
        out_specs=(P(None, "modes", "axial", "sector", None), P("axial", "sector", None)),
        check_vma=False,
    )
```

```python
import functools

import jax
import jax.numpy as jnp
from jax import lax
from jax.experimental import pallas as pl
from jax.experimental.pallas import tpu as pltpu
from jax.sharding import PartitionSpec as P

ITERS = 2
RELAX = 0.6
CAP = 96
LANES = 128
MESH = pl.DeviceIdType.MESH
BF16 = jnp.bfloat16
F32 = jnp.float32
I32 = jnp.int32


def one_hot(flags):
    return jnp.where(flags, 1.0, 0.0).astype(BF16)


def halves(values):
    high = values.astype(BF16)
    return high, (values - high.astype(F32)).astype(BF16)


def dot_nt(left, right):
    return lax.dot_general(
        left, right, (((1,), (1,)), ((), ())), preferred_element_type=F32
    )


def read(ref, *index):
    *lead, at = index
    tiles = ref.shape[len(lead)]
    return jnp.concatenate([ref[(*lead, i, at)] for i in range(tiles)], axis=-1)


def write(ref, *index_and_value):
    *lead, at, value = index_and_value
    for i in range(ref.shape[len(lead)]):
        ref[(*lead, i, at)] = value[..., i * LANES : (i + 1) * LANES]


def flip(sector, mask, n_sector):
    bit = 1
    other = sector
    while bit < n_sector:
        if mask & bit:
            other = other + bit * (1 - 2 * (sector // bit % 2))
        bit *= 2
    return other


def partner_order(n_sector):
    hops = {mask: (0, 1, 2, 1)[mask // 2 % 4] + mask // 8 for mask in range(n_sector)}
    return sorted(range(n_sector), key=lambda mask: (hops[mask], mask))


def kernel(
    n_sector,
    n_axial,
    shape,
    rhs_hbm,
    start_hbm,
    sound_hbm,
    direct_hbm,
    omega_hbm,
    gain_hbm,
    phase_hbm,
    bin_hbm,
    source_hbm,
    sector_hbm,
    target_hbm,
    adjoint,
    sens_sum,
    scale,
    slot_sum,
    put_row,
    put_radial,
    rhs,
    field_a,
    field_b,
    sound,
    direct,
    omega,
    gain,
    phase,
    bins,
    source,
    sector,
    target,
    base,
    k_axial,
    k_rest,
    edge,
    pick_radial,
    pick_row,
    picked_start,
    picked_base,
    edge_pick,
    lane_hot,
    block_hot,
    gain_cos,
    gain_sin,
    put_edge,
    match,
    sound_send,
    sound_side,
    side_send,
    side_recv,
    end_send,
    end_recv,
    sound_end,
    cell_send,
    cell_recv,
    flame_send,
    flame_recv,
    direct_tiles,
    slot_direct,
    sens_own,
    sens_other,
    edge_own,
    edge_other,
    slot_own,
    slot_other,
    in_sem,
    sound_sems,
    halo_sems,
    cell_sems,
    flame_sems,
    sens_sems,
):
    modes, axial_cells, azimuth_cells, radial_cells = shape
    channels = 2 * modes
    rows = axial_cells * azimuth_cells
    flames = gain.shape[1]
    tiles = radial_cells // LANES
    half_blocks = n_sector // 2
    half = half_blocks * CAP
    near, far = 0, 1
    axial = lax.axis_index("axial")
    my_sector = lax.axis_index("sector")
    my_modes = lax.axis_index("modes")
    up_axial = lax.rem(axial + 1, n_axial)
    down_axial = lax.rem(axial + n_axial - 1, n_axial)
    next_sector = lax.rem(my_sector + 1, n_sector)
    last_sector = lax.rem(my_sector + n_sector - 1, n_sector)
    partners = [flip(my_sector, mask, n_sector) for mask in partner_order(n_sector)]

    barrier = pltpu.get_barrier_semaphore()
    for other in partners[1:]:
        pl.semaphore_signal(barrier, inc=1, device_id={"sector": other}, device_id_type=MESH)
    for other in (next_sector, last_sector):
        pl.semaphore_signal(barrier, inc=1, device_id={"sector": other}, device_id_type=MESH)
    for other in (up_axial, down_axial):
        pl.semaphore_signal(barrier, inc=1, device_id={"axial": other}, device_id_type=MESH)
    pl.semaphore_signal(
        barrier, inc=1, device_id={"modes": 1 - my_modes}, device_id_type=MESH
    )

    inner = pl.ds(azimuth_cells, rows)
    pieces = [pl.ds(i * LANES, LANES) for i in range(tiles)]
    loads = {}
    for name, source_ref, target_ref in (
        [("sector", sector_hbm, sector), ("target", target_hbm, target), ("source", source_hbm, source)]
        + [("bins", bin_hbm, bins), ("phase", phase_hbm, phase), ("gain", gain_hbm, gain)]
        + [(("sound", i), sound_hbm.at[:, pieces[i]], sound.at[i, inner]) for i in range(tiles)]
        + [(("start", i), start_hbm.at[:, :, pieces[i]], field_a.at[:, i, inner]) for i in range(tiles)]
        + [("omega", omega_hbm, omega), ("rhs", rhs_hbm, rhs), ("direct", direct_hbm, direct)]
    ):
        loads[name] = pltpu.make_async_copy(source_ref, target_ref, in_sem.at[len(loads)])
        if name not in ("rhs", "direct"):
            loads[name].start()

    def loaded(*names):
        for name in names:
            loads[name].wait()

    loaded("sector", "target", "source")
    partner = jnp.zeros((n_sector, LANES), I32)
    position = lax.broadcasted_iota(I32, (n_sector, LANES), 0)
    for p, other in enumerate(partners):
        partner = jnp.where(position == p, other, partner)
    partner = jnp.concatenate([partner] * (flames // LANES), axis=1)
    in_block = jnp.where(jnp.broadcast_to(sector[...], (n_sector, flames)) == partner, 1.0, 0.0)
    block_hot[...] = in_block
    before = one_hot(
        lax.broadcasted_iota(I32, (flames, flames), 0)
        < lax.broadcasted_iota(I32, (flames, flames), 1)
    )
    earlier = jnp.dot(in_block.astype(BF16), before, preferred_element_type=F32)
    rank = jnp.sum(in_block * earlier, axis=0, keepdims=True).astype(I32)
    block_of = jnp.sum(
        in_block * lax.broadcasted_iota(I32, (n_sector, flames), 0).astype(F32),
        axis=0,
        keepdims=True,
    ).astype(I32)
    lane = (rank + CAP * block_of) & (LANES - 1)
    lane_hot[...] = one_hot(
        lax.broadcasted_iota(I32, (LANES, flames), 0) == jnp.broadcast_to(lane, (LANES, flames))
    )

    def pack(parts):
        left = jnp.concatenate(
            [
                jnp.concatenate(
                    [part * block_hot[p : p + 1, :] for p in range(n_sector)], axis=0
                ).astype(BF16)
                for part in parts
            ],
            axis=0,
        )
        packed = dot_nt(left, lane_hot[...])
        total = packed[: 8 * n_sector]
        for i in range(1, len(parts)):
            total = total + packed[8 * n_sector * i : 8 * n_sector * (i + 1)]
        return total.reshape(n_sector, 8, LANES)

    target_row = (target[...] // radial_cells).astype(F32)
    target_radial = (target[...] % radial_cells).astype(F32)
    sub = lax.broadcasted_iota(I32, (8, flames), 0)
    cell_send[...] = pack(
        [
            jnp.where(
                sub == 0,
                jnp.broadcast_to(target_row, (8, flames)),
                jnp.where(sub == 1, jnp.broadcast_to(target_radial, (8, flames)), 0.0),
            )
        ]
    )

    def remote(src, dst, send_sem, recv_sem, device):
        return pltpu.make_async_remote_copy(
            src_ref=src,
            dst_ref=dst,
            send_sem=send_sem,
            recv_sem=recv_sem,
            device_id=device,
            device_id_type=MESH,
        )

    def wait_bytes(ref, sem):
        pltpu.make_async_copy(ref, ref, sem).wait()

    first_rows = pl.ds(azimuth_cells, azimuth_cells)
    last_rows = pl.ds(rows, azimuth_cells)
    sent = []

    def start_sides(send, recv, sems):
        remote(send.at[1], recv.at[0], sems.at[0, 0], sems.at[1, 0], {"sector": next_sector}).start()
        remote(send.at[0], recv.at[1], sems.at[0, 0], sems.at[1, 0], {"sector": last_sector}).start()
        sent.append((recv, sems.at[0, 0]))

    def start_ends(first, last, recv, sems):
        remote(last, recv.at[0], sems.at[0, 1], sems.at[1, 1], {"axial": up_axial}).start()
        remote(first, recv.at[1], sems.at[0, 1], sems.at[1, 1], {"axial": down_axial}).start()
        sent.append((recv, sems.at[0, 1]))

    def start_blocks(send, recv, sems):
        for p in reversed(range(1, n_sector)):
            group = 0 if p < half_blocks else 1
            remote(
                send.at[p], recv.at[p], sems.at[2], sems.at[group], {"sector": partners[p]}
            ).start()
        sent.append((send.at[pl.ds(1, n_sector - 1)], sems.at[2]))

    def wait_blocks(recv, sems, group):
        start = max(1, group * half_blocks)
        wait_bytes(recv.at[pl.ds(start, (group + 1) * half_blocks - start)], sems.at[group])

    def start_partner(send, recv, i):
        remote(
            send, recv, sens_sems.at[0, i], sens_sems.at[1, i], {"modes": 1 - my_modes}
        ).start()
        sent.append((send, sens_sems.at[0, i]))

    side_rows = [
        pl.ds(row, axial_cells, azimuth_cells) for row in (0, azimuth_cells - 1)
    ]
    padded_side_rows = [
        pl.ds(azimuth_cells + row, axial_cells, azimuth_cells) for row in (0, azimuth_cells - 1)
    ]

    loaded(*[("sound", i) for i in range(tiles)])
    for side in range(2):
        for i in range(tiles):
            sound_send[side, i] = sound[i, padded_side_rows[side], :]

    pl.semaphore_wait(barrier, n_sector + 4)

    start_blocks(cell_send, cell_recv, cell_sems)
    start_ends(sound.at[:, first_rows], sound.at[:, last_rows], sound_end, sound_sems)
    start_sides(sound_send, sound_side, sound_sems)
    cell_recv[0] = cell_send[0]

    loaded(*[("start", i) for i in range(tiles)])
    loads["rhs"].start()
    sems = halo_sems.at[0]
    for side in range(2):
        for c in range(channels):
            for i in range(tiles):
                side_send[0, side, c, i] = field_a[c, i, padded_side_rows[side], :]
    start_sides(side_send.at[0], side_recv.at[0], sems)
    start_ends(field_a.at[:, :, first_rows], field_a.at[:, :, last_rows], end_recv.at[0], sems)

    cell = source[...]
    row_of = jnp.broadcast_to(cell // radial_cells, (rows, flames))
    pick_row[...] = jnp.where(lax.broadcasted_iota(I32, (rows, flames), 0) == row_of, 1.0, 0.0)
    radial_of = jnp.broadcast_to(cell % radial_cells, (radial_cells, flames))
    radial_hot = one_hot(lax.broadcasted_iota(I32, (radial_cells, flames), 0) == radial_of)
    pick_radial[:radial_cells] = radial_hot
    pick_radial[radial_cells:] = radial_hot

    loaded("bins", "phase", "gain")
    bin_count = phase.shape[1]
    bin_hot = jnp.where(
        lax.broadcasted_iota(I32, (bin_count, flames), 0)
        == jnp.broadcast_to(bins[...], (bin_count, flames)),
        1.0,
        0.0,
    )
    angle = phase[...]
    gains = jnp.broadcast_to(gain[...], (modes, flames))
    exact = lax.Precision.HIGHEST
    gain_cos[...] = gains * jnp.dot(
        jnp.cos(angle), bin_hot, precision=exact, preferred_element_type=F32
    )
    gain_sin[...] = -gains * jnp.dot(
        jnp.sin(angle), bin_hot, precision=exact, preferred_element_type=F32
    )

    def pick(planes, hot=pick_row):
        high, low = halves(jnp.concatenate(planes, axis=0))
        columns = jnp.dot(
            jnp.concatenate([high, low], axis=1), pick_radial[...], preferred_element_type=F32
        ).reshape(len(planes), hot.shape[0], flames)
        return jnp.sum(columns * hot[...][None], axis=1)

    def pick_field(ref, at):
        return jnp.concatenate(
            [
                pick([read(ref, g * modes + m, at) for m in range(modes)])
                for g in range(2)
            ],
            axis=0,
        )

    def send_flames(picked, step):
        real, imag = picked[:modes], picked[modes:]
        cosines, sines = gain_cos[...], gain_sin[...]
        amounts = jnp.concatenate(
            [cosines * real - sines * imag, cosines * imag + sines * real], axis=0
        )
        high = amounts.astype(BF16).astype(F32)
        flame_send[step] = pack([high, amounts - high])
        start_blocks(flame_send.at[step], flame_recv.at[step], flame_sems.at[step])
        flame_recv[step, 0] = flame_send[step, 0]

    picked_start[...] = pick_field(field_a, inner)
    send_flames(picked_start[...], 0)

    tile = (azimuth_cells, radial_cells)
    azimuth = lax.broadcasted_iota(I32, tile, 0)
    radial = lax.broadcasted_iota(I32, tile, 1)

    def own_rows(a):
        if isinstance(a, int):
            return pl.ds(a * azimuth_cells, azimuth_cells)
        return pl.ds(pl.multiple_of(a * azimuth_cells, azimuth_cells), azimuth_cells)

    def couplings(a, _):
        s = read(sound, own_rows(a + 1))
        at = own_rows(a)
        k_rest[0, at, :] = jnp.where(azimuth == 0, 0.0, 0.5 * (s + pltpu.roll(s, 1, 0)))
        k_rest[1, at, :] = jnp.where(
            azimuth == azimuth_cells - 1, 0.0, 0.5 * (s + pltpu.roll(s, azimuth_cells - 1, 0))
        )
        k_rest[2, at, :] = jnp.where(radial == 0, 0.0, 0.5 * (s + pltpu.roll(s, 1, 1)))
        k_rest[3, at, :] = jnp.where(
            radial == radial_cells - 1, 0.0, 0.5 * (s + pltpu.roll(s, radial_cells - 1, 1))
        )
        return 0

    def axial_coupling(a, _):
        k_axial[own_rows(a), :] = 0.5 * (read(sound, own_rows(a)) + read(sound, own_rows(a + 1)))
        return 0

    lax.fori_loop(0, axial_cells, couplings, 0, unroll=True)
    lax.fori_loop(1, axial_cells, axial_coupling, 0, unroll=True)

    loaded("omega", "rhs")
    loads["direct"].start()
    omega_real = [omega[0, m] for m in range(modes)]
    omega_imag = [omega[1, m] for m in range(modes)]

    def base_rows(field, a, modes_here):
        low, high = a > 0, a < axial_cells - 1
        at, mid, top = own_rows(a), own_rows(a + 1), own_rows(a + 2)
        k_slo, k_shi, k_rlo, k_rhi = (k_rest[i, at, :] for i in range(4))
        k_alo = k_axial[at, :] if low else None
        k_ahi = k_axial[mid, :] if high else None
        for m in modes_here:
            real, imag = read(field, m, mid), read(field, modes + m, mid)
            for c, x, mass in (
                (m, real, omega_real[m] * real - omega_imag[m] * imag),
                (modes + m, imag, omega_real[m] * imag + omega_imag[m] * real),
            ):
                total = rhs[c, at, :] + mass
                if low:
                    total = total + k_alo * read(field, c, at)
                if high:
                    total = total + k_ahi * read(field, c, top)
                total = total + k_slo * pltpu.roll(x, 1, 0)
                total = total + k_shi * pltpu.roll(x, azimuth_cells - 1, 0)
                total = total + k_rlo * pltpu.roll(x, 1, 1)
                total = total + k_rhi * pltpu.roll(x, radial_cells - 1, 1)
                write(base, c, at, total)

    def make_base(field, low, high):
        for a in range(low, high):
            base_rows(field, a, range(modes))

    first_axial = axial == 0
    last_axial = axial == n_axial - 1
    first, last = pl.ds(0, azimuth_cells), pl.ds(rows - azimuth_cells, azimuth_cells)
    whole = pl.ds(0, azimuth_cells)

    edge_rows = 2 * axial_cells + 2 * azimuth_cells

    def signed_sum(terms):
        return sum(terms[1:modes], terms[0]) - sum(terms[modes + 1 :], terms[modes])

    def add_halo(step):
        wait_bytes(end_recv.at[step], halo_sems.at[step, 1, 1])
        k_low = k_axial[pl.ds(0, azimuth_cells), :]
        k_high = k_axial[pl.ds(rows, azimuth_cells), :]
        low_terms, high_terms, planes = [], [], [[] for _ in range(channels)]
        for c in range(channels):
            below = k_low * jnp.where(first_axial, 0.0, read(end_recv, step, 0, c, whole))
            above = k_high * jnp.where(last_axial, 0.0, read(end_recv, step, 1, c, whole))
            write(base, c, first, read(base, c, first) + below)
            write(base, c, last, read(base, c, last) + above)
            planes[c] += [below, above]
            if step == ITERS - 1:
                low_terms.append(below * read(direct_tiles, c, first))
                high_terms.append(above * read(direct_tiles, c, last))
        wait_bytes(side_recv.at[step], halo_sems.at[step, 1, 0])
        for side in range(2):
            at = side_rows[side]
            sides = [[] for _ in range(channels)]
            for i in range(tiles):
                terms = []
                for c in range(channels):
                    added = edge[side, i] * side_recv[step, side, c, i]
                    sides[c].append(added)
                    base[c, i, at, :] = base[c, i, at, :] + added
                    if step == ITERS - 1:
                        terms.append(added * direct_tiles[c, i, at, :])
                if step == ITERS - 1:
                    edge_own[i, pl.ds(side * axial_cells, axial_cells), :] = scale[
                        i, at, :
                    ] * signed_sum(terms)
            for c in range(channels):
                planes[c].insert(side, jnp.concatenate(sides[c], axis=1))
        if step < ITERS - 1:
            return [jnp.concatenate(parts, axis=0) for parts in planes]
        if step == ITERS - 1:
            for end, at, terms in ((0, first, low_terms), (1, last, high_terms)):
                write(
                    edge_own,
                    pl.ds(2 * axial_cells + end * azimuth_cells, azimuth_cells),
                    read(scale, at) * signed_sum(terms),
                )

    all_rows = pl.ds(0, rows)
    real_base, imag_base = [], []
    for m in range(modes):
        for a in range(axial_cells):
            base_rows(field_a, a, [m])
        pair = pick([read(base, m, all_rows), read(base, modes + m, all_rows)])
        real_base.append(pair[0:1])
        imag_base.append(pair[1:2])
    picked_base[...] = jnp.concatenate(real_base + imag_base, axis=0)

    def squeeze(recv, group):
        lanes = lax.broadcasted_iota(I32, (8, LANES), 1)
        parts = []
        for start_block in range(group * half_blocks, (group + 1) * half_blocks, 4):
            b = [recv[start_block + i] for i in range(4)]
            parts.append(jnp.where(lanes < 96, b[0], b[1]))
            parts.append(jnp.where(lanes < 64, b[1], b[2]))
            parts.append(jnp.where(lanes < 32, b[2], b[3]))
        return jnp.concatenate(parts, axis=1)

    def put_hots(group):
        cells = squeeze(cell_recv, group)
        row, column = cells[0:1], cells[1:2]
        put_row[group] = one_hot(
            lax.broadcasted_iota(I32, (rows, half), 0).astype(F32)
            == jnp.broadcast_to(row, (rows, half))
        )
        upright = jnp.broadcast_to(column, (LANES, half)).T
        put_radial[group] = one_hot(
            jnp.concatenate([upright] * tiles, axis=1)
            == lax.broadcasted_iota(I32, (half, radial_cells), 1).astype(F32)
        )
        return row, column

    def add_flames(parts, hot, group):
        left = jnp.concatenate(
            [hot * part[c : c + 1, :] for part in parts for c in range(channels)], axis=0
        )
        totals = jnp.dot(left, put_radial[group], preferred_element_type=F32)
        middle = totals.shape[0] // 2
        return totals[:middle] + totals[middle:]

    chunk = rows // 4

    i = lax.broadcasted_iota(I32, (edge_rows, LANES), 0)
    edge_row = jnp.where(
        i < axial_cells,
        i * azimuth_cells,
        jnp.where(
            i < 2 * axial_cells,
            (i - axial_cells) * azimuth_cells + azimuth_cells - 1,
            jnp.where(
                i < 2 * axial_cells + azimuth_cells,
                i - 2 * axial_cells,
                i - 2 * axial_cells - 2 * azimuth_cells + rows,
            ),
        ),
    ).astype(F32)
    flame_row = (cell // radial_cells).astype(F32)
    edge_pick[...] = jnp.where(
        jnp.concatenate([edge_row] * (flames // LANES), axis=1)
        == jnp.broadcast_to(flame_row, (edge_rows, flames)),
        1.0,
        0.0,
    )

    def all_hots(group):
        row, column = put_hots(group)
        put_edge[group] = one_hot(
            jnp.concatenate([edge_row] * (half // LANES), axis=1)
            == jnp.broadcast_to(row, (edge_rows, half))
        )
        upright = jnp.broadcast_to(row * radial_cells + column, (LANES, half)).T
        match[group] = one_hot(
            jnp.concatenate([upright] * (flames // LANES), axis=1)
            == jnp.broadcast_to(cell.astype(F32), (half, flames))
        )

    def found_at_flames(parts, group):
        found = jnp.dot(jnp.concatenate(parts, axis=0), match[group], preferred_element_type=F32)
        return found[:channels] + found[channels:]

    wait_blocks(cell_recv, cell_sems, near)
    all_hots(near)

    wait_bytes(sound_end, sound_sems.at[1, 1])
    wait_bytes(sound_side, sound_sems.at[1, 0])
    k_axial[first, :] = 0.5 * (
        read(sound, first_rows) + jnp.where(first_axial, 0.0, read(sound_end, 0, whole))
    )
    k_axial[pl.ds(rows, azimuth_cells), :] = 0.5 * (
        read(sound, last_rows) + jnp.where(last_axial, 0.0, read(sound_end, 1, whole))
    )
    for side in range(2):
        for i in range(tiles):
            edge[side, i] = 0.5 * (sound[i, padded_side_rows[side], :] + sound_side[side, i])

    def scales(a, _):
        at = own_rows(a)
        low = jnp.broadcast_to(read(edge, 0, pl.ds(a, 1)), tile)
        high = jnp.broadcast_to(read(edge, 1, pl.ds(a, 1)), tile)
        weights = k_axial[at, :] + k_axial[own_rows(a + 1), :] + k_rest[2, at, :] + k_rest[3, at, :]
        weights = weights + jnp.where(azimuth == 0, low, k_rest[0, at, :])
        weights = weights + jnp.where(azimuth == azimuth_cells - 1, high, k_rest[1, at, :])
        write(scale, at, RELAX / weights)
        return 0

    lax.fori_loop(0, axial_cells, scales, 0, unroll=True)
    picked_scale = pick([read(scale, all_rows)])

    wait_blocks(cell_recv, cell_sems, far)
    all_hots(far)
    wait_blocks(flame_recv.at[0], flame_sems.at[0], near)
    near_parts = halves(squeeze(flame_recv.at[0], near))
    found_near = found_at_flames(near_parts, near)
    planes = add_halo(0)
    inside = picked_base[...] - found_near + pick(planes, edge_pick)

    edge_totals = add_flames(near_parts, put_edge[near], near)

    wait_blocks(flame_recv.at[0], flame_sems.at[0], far)
    parts = halves(squeeze(flame_recv.at[0], far))
    totals = edge_totals + add_flames(parts, put_edge[far], far)
    sems = halo_sems.at[1]
    for c in range(channels):
        here = c * edge_rows
        for side in range(2):
            for i in range(tiles):
                added = totals[
                    here + side * axial_cells : here + (side + 1) * axial_cells,
                    i * LANES : (i + 1) * LANES,
                ]
                side_send[1, side, c, i] = (1.0 - RELAX) * side_send[0, side, c, i] + scale[
                    i, side_rows[side], :
                ] * (base[c, i, side_rows[side], :] - added)
    start_sides(side_send.at[1], side_recv.at[1], sems)
    for c in range(channels):
        here = c * edge_rows + 2 * axial_cells
        for end, at, padded_at in ((0, first, first_rows), (1, last, last_rows)):
            added = totals[here + end * azimuth_cells : here + (end + 1) * azimuth_cells]
            write(
                end_send,
                end,
                c,
                pl.ds(0, azimuth_cells),
                (1.0 - RELAX) * read(field_a, c, padded_at)
                + read(scale, at) * (read(base, c, at) - added),
            )
    start_ends(end_send.at[0], end_send.at[1], end_recv.at[1], sems)

    picked = (1.0 - RELAX) * picked_start[...] + picked_scale * (
        inside - found_at_flames(parts, far)
    )
    send_flames(picked, 1)

    loaded("direct")
    chunk_cells = chunk // azimuth_cells

    def send_sensitivity(top):
        at = pl.ds(top, chunk)
        padded_at = pl.ds(top + azimuth_cells, chunk)
        terms = []
        for c in range(channels):
            weight = direct[c, at, :].astype(F32)
            write(direct_tiles, c, at, weight)
            terms.append(
                weight
                * ((1.0 - RELAX) * read(field_b, c, padded_at) + read(scale, at) * read(base, c, at))
            )
        write(sens_own, at, signed_sum(terms))
        start_partner(sens_own.at[:, at], sens_other.at[:, at], 0)

    done = 0
    for top in range(0, rows, chunk):
        totals = add_flames(near_parts, put_row[near, top : top + chunk, :], near)
        totals = totals + add_flames(parts, put_row[far, top : top + chunk, :], far)
        at = pl.ds(top, chunk)
        padded_at = pl.ds(top + azimuth_cells, chunk)
        for c in range(channels):
            write(
                field_b,
                c,
                padded_at,
                (1.0 - RELAX) * read(field_a, c, padded_at)
                + read(scale, at) * (read(base, c, at) - totals[c * chunk : (c + 1) * chunk]),
            )
        ready = (top + chunk) // azimuth_cells
        ready = axial_cells if ready == axial_cells else ready - 1
        make_base(field_b, done, ready)
        done = ready
        if top:
            send_sensitivity(top - chunk)
    send_sensitivity(rows - chunk)

    def direct_at_slots(group):
        hot = put_row[group].astype(F32)
        for g in range(2):
            columns = dot_nt(
                direct[g * modes : (g + 1) * modes].reshape(modes * rows, radial_cells),
                put_radial[group],
            ).reshape(modes, rows, half)
            slot_direct[group, g * modes : (g + 1) * modes] = jnp.sum(columns * hot[None], axis=1)

    direct_at_slots(near)
    direct_at_slots(far)
    add_halo(1)
    start_partner(edge_own, edge_other, 2)
    parts = []
    for group in (near, far):
        wait_blocks(flame_recv.at[1], flame_sems.at[1], group)
        amounts = squeeze(flame_recv.at[1], group)
        products = amounts * slot_direct[group]
        slot_own[group] = jnp.sum(products[:modes], axis=0, keepdims=True) - jnp.sum(
            products[modes:], axis=0, keepdims=True
        )
        parts.append(halves(amounts))
    start_partner(slot_own, slot_other, 1)
    for top in range(0, rows, chunk):
        totals = add_flames(parts[near], put_row[near, top : top + chunk, :], near)
        totals = totals + add_flames(parts[far], put_row[far, top : top + chunk, :], far)
        at = pl.ds(top, chunk)
        padded_at = pl.ds(top + azimuth_cells, chunk)
        for c in range(channels):
            adjoint[c, at, :] = (1.0 - RELAX) * read(field_b, c, padded_at) + read(scale, at) * (
                read(base, c, at) - totals[c * chunk : (c + 1) * chunk]
            )

    wait_bytes(sens_other, sens_sems.at[1, 0])
    write(sens_sum, all_rows, read(sens_own, all_rows) + read(sens_other, all_rows))
    wait_bytes(edge_other, sens_sems.at[1, 2])
    edges = [edge_own[i] + edge_other[i] for i in range(tiles)]
    for i in range(tiles):
        for end, at in ((0, first), (1, last)):
            low = 2 * axial_cells + end * azimuth_cells
            sens_sum[i, at, :] = sens_sum[i, at, :] + edges[i][low : low + azimuth_cells]
        for side in range(2):
            at = side_rows[side]
            sens_sum[i, at, :] = (
                sens_sum[i, at, :] + edges[i][side * axial_cells : (side + 1) * axial_cells]
            )
    wait_bytes(slot_other, sens_sems.at[1, 1])
    slot_sum[...] = slot_own[...] + slot_other[...]
    for ref, sem in sent:
        wait_bytes(ref, sem)


def hand_over(
    adjoint,
    sens_sum,
    scale,
    slot_sum,
    put_row,
    put_radial,
    adjoint_out,
    sensitivity_out,
    sensitivity,
    sems,
):
    rows = put_row.shape[1]
    adjoint_copy = pltpu.make_async_copy(adjoint, adjoint_out, sems.at[0])
    adjoint_copy.start()
    slot_totals = 0.0
    for group in range(2):
        left = jnp.concatenate(
            [put_row[group] * part for part in halves(slot_sum[group])], axis=0
        )
        totals = jnp.dot(left, put_radial[group], preferred_element_type=F32)
        slot_totals = slot_totals + totals[:rows] + totals[rows:]
    all_rows = pl.ds(0, rows)
    sensitivity[...] = read(sens_sum, all_rows) - read(scale, all_rows) * slot_totals
    sensitivity_copy = pltpu.make_async_copy(sensitivity, sensitivity_out, sems.at[1])
    sensitivity_copy.start()
    sensitivity_copy.wait()
    adjoint_copy.wait()


def local(
    n_sector,
    n_axial,
    rhs,
    adjoint_start,
    sound_sq,
    direct_mode,
    omega_sq,
    flame_gain,
    delay_phase,
    delay_bin,
    flame_cell,
    injector_sector,
    injector_cell,
):
    parts, modes, axial_cells, azimuth_cells, radial_cells = rhs.shape
    channels = parts * modes
    rows = axial_cells * azimuth_cells
    flames = flame_cell.shape[1]
    half = n_sector // 2 * CAP
    tiles = radial_cells // LANES
    block = (channels, rows, radial_cells)
    padded = (channels, tiles, rows + 2 * azimuth_cells, LANES)
    side = (tiles, axial_cells, LANES)
    plane = (rows, radial_cells)
    dma = pltpu.SemaphoreType.DMA
    vmem = pltpu.VMEM
    scratch = [
        vmem(block, F32),
        vmem(padded, F32),
        vmem(padded, F32),
        vmem(padded[1:], F32),
        vmem(block, BF16),
        pltpu.SMEM((2, modes), F32),
        vmem((1, flames), F32),
        vmem(delay_phase.shape, F32),
        vmem((1, flames), I32),
        vmem((1, flames), I32),
        vmem((1, flames), I32),
        vmem((1, flames), I32),
        vmem((channels, tiles, rows, LANES), F32),
        vmem((rows + azimuth_cells, radial_cells), F32),
        vmem((4,) + plane, F32),
        vmem((2,) + side, F32),
        vmem((2 * radial_cells, flames), BF16),
        vmem((rows, flames), F32),
        vmem((channels, flames), F32),
        vmem((channels, flames), F32),
        vmem((2 * (axial_cells + azimuth_cells), flames), F32),
        vmem((LANES, flames), BF16),
        vmem((n_sector, flames), F32),
        vmem((modes, flames), F32),
        vmem((modes, flames), F32),
        vmem((2, 2 * (axial_cells + azimuth_cells), half), BF16),
        vmem((2, half, flames), BF16),
        vmem((2,) + side, F32),
        vmem((2,) + side, F32),
        vmem((ITERS, 2, channels) + side, F32),
        vmem((ITERS, 2, channels) + side, F32),
        vmem((2, channels, tiles, azimuth_cells, LANES), F32),
        vmem((ITERS, 2, channels, tiles, azimuth_cells, LANES), F32),
        vmem((2, tiles, azimuth_cells, LANES), F32),
        vmem((n_sector, 8, LANES), F32),
        vmem((n_sector, 8, LANES), F32),
        vmem((ITERS, n_sector, 8, LANES), F32),
        vmem((ITERS, n_sector, 8, LANES), F32),
        vmem((channels, tiles, rows, LANES), F32),
        vmem((2, channels, half), F32),
        vmem((tiles, rows, LANES), F32),
        vmem((tiles, rows, LANES), F32),
        vmem((tiles, 2 * (axial_cells + azimuth_cells), LANES), F32),
        vmem((tiles, 2 * (axial_cells + azimuth_cells), LANES), F32),
        vmem((2, 1, half), F32),
        vmem((2, 1, half), F32),
        dma((9 + 2 * tiles,)),
        dma((2, 2)),
        dma((ITERS, 2, 2)),
        dma((3,)),
        dma((ITERS, 3)),
        dma((2, 3)),
    ]
    in_hbm = pl.BlockSpec(memory_space=pltpu.HBM)

    def stay(array):
        return pltpu.with_memory_space_constraint(array, pltpu.HBM)

    in_vmem = pl.BlockSpec(memory_space=pltpu.VMEM)
    results = pl.pallas_call(
        functools.partial(
            kernel, n_sector, n_axial, (modes, axial_cells, azimuth_cells, radial_cells)
        ),
        out_shape=(
            jax.ShapeDtypeStruct(block, F32),
            jax.ShapeDtypeStruct((tiles, rows, LANES), F32),
            jax.ShapeDtypeStruct((tiles, rows, LANES), F32),
            jax.ShapeDtypeStruct((2, 1, half), F32),
            jax.ShapeDtypeStruct((2, rows, half), BF16),
            jax.ShapeDtypeStruct((2, half, radial_cells), BF16),
        ),
        in_specs=[in_hbm] * 11,
        out_specs=(in_vmem,) * 6,
        scratch_shapes=scratch,
        compiler_params=pltpu.CompilerParams(
            collective_id=0, has_side_effects=True, vmem_limit_bytes=40 * 1024 * 1024
        ),
        name="helmholtz_steps",
    )(
        stay(rhs.reshape(block)),
        stay(adjoint_start.reshape(block)),
        stay(sound_sq.reshape(plane)),
        stay(direct_mode.reshape(block)),
        stay(omega_sq),
        stay(flame_gain),
        stay(delay_phase),
        stay(delay_bin),
        stay(flame_cell),
        stay(injector_sector.reshape(1, flames)),
        stay(injector_cell),
    )
    adjoint, sensitivity = pl.pallas_call(
        hand_over,
        out_shape=(jax.ShapeDtypeStruct(block, F32), jax.ShapeDtypeStruct(plane, F32)),
        in_specs=[in_vmem] * 6,
        out_specs=(in_hbm, in_hbm),
        scratch_shapes=[vmem(plane, F32), dma((2,))],
        compiler_params=pltpu.CompilerParams(vmem_limit_bytes=20 * 1024 * 1024),
        name="hand_over",
    )(*[pltpu.with_memory_space_constraint(result, pltpu.VMEM) for result in results])
    return adjoint.reshape(rhs.shape), sensitivity.reshape(sound_sq.shape)


def solution(mesh):
    placed = (
        P(None, "modes", "axial", "sector", None),
        P(None, "modes", "axial", "sector", None),
        P("axial", "sector", None),
        P(None, "modes", "axial", "sector", None),
        P(None, "modes"),
        P("axial", "sector"),
        P("modes", None),
        P("axial", "sector"),
        P("axial", "sector"),
        P("axial", "sector", None),
        P("axial", "sector"),
    )
    return jax.shard_map(
        functools.partial(local, mesh.shape["sector"], mesh.shape["axial"]),
        mesh=mesh,
        in_specs=placed,
        out_specs=(P(None, "modes", "axial", "sector", None), P("axial", "sector", None)),
        check_vma=False,
    )
```
